256 devices in a mesh: tile: 32 (over y, x, core), cls: 8 (over z).
Axes of the slice: x: 4, y: 4, z: 8, core: 2. Of those that a mesh axis runs over, the one named last changes fastest.
Arguments:
- subvols: bfloat16 [8192, 32768], P(('tile', 'cls')), may hold values from -16 to 16
- tomogram: int32 [8192, 1], P(('tile', 'cls')), may hold values from 0 to 31; in each aligned block of 32 rows (0 to 31, 32 to 63, ...) at most 2 rows name the same one
- sharpness: bfloat16 [8192], P(('tile', 'cls')), may hold values from 0.5 to 6
- references: bfloat16 [8, 32768], P('cls'), may hold values from -6 to 6
- interp: bfloat16 [4, 3, 32, 32], replicated, may hold values from -0.4 to 1.1
- weighting: bfloat16 [32, 4, 32768], P('tile'), may hold values from 0.099609375 to 1
Outputs:
- updated: bfloat16 [8, 32768], P('cls')
- posterior: float32 [8192, 8], P(('tile', 'cls'))
The draws below stay inside these ranges and needn't reach their ends.
Inputs may be any that keep to these rules, and one draw needn't show every extreme that they name: In the rows of one device no tomogram appears more than 2 times, and some tomogram exactly that many times.
All inputs are finite; a program needn't handle non-finite values.
Results may differ from the reference program's by a relative error of at most 0.03.
Values may be sent and summed in bfloat16 or wider, within the bound.
A program may use at most 128 MiB of HBM per device.

```python
import math
import jax
import jax.numpy as jnp
import numpy as np
from jax import lax

EDGE = 32
VOXELS = 32768
SUB_DEV = 32
ORIENTS = 4
ITERS = 1
REFS = 8
TOMOS = 32
CAPACITY = 2
SUBVOLS = 8192
N_TILE = 32
N_CLS = 8
DEVICES = 256


def shared_volumes(key):
    return jnp.clip(jax.random.normal(jax.random.fold_in(key, 101), (REFS, VOXELS), jnp.float32), -6.0, 6.0)


def draw_references(key, part):
    base = shared_volumes(key)
    return base.astype(jnp.bfloat16)


def draw_subvols(key, part):
    key = jax.random.fold_in(key, 7)
    noise = jnp.clip(jax.random.normal(key, (SUBVOLS, VOXELS), jnp.float32), -6.0, 6.0)
    values = noise
    return jnp.clip(values, -16.0, 16.0).astype(jnp.bfloat16)


def draw_sharpness(key, part):
    key = jax.random.fold_in(key, 11)
    lowest, highest = (math.log(0.5), math.log(6.0))
    values = jnp.exp(jax.random.uniform(key, (SUBVOLS,), jnp.float32, lowest, highest))
    return values.astype(jnp.bfloat16)


def draw_interp(key, part):
    key = jax.random.fold_in(key, 23)
    shape = (ORIENTS, 3, EDGE, EDGE)
    noise = jnp.clip(jax.random.normal(key, shape, jnp.float32), -6.0, 6.0)
    values = 0.7 * jnp.eye(EDGE, dtype=jnp.float32) + noise * (0.3 / math.sqrt(EDGE))
    return values.astype(jnp.bfloat16)


def levels(own_key, dims, pieces, smallest, largest):
    loudness, own = 1.0, jax.random.fold_in(own_key, 6)
    for dim, blocks in pieces:
        draws = jnp.exp(jax.random.uniform(jax.random.fold_in(own, dim), (blocks,), jnp.float32, smallest / len(pieces), largest / len(pieces)))
        loudness = loudness * jnp.repeat(draws, dims[dim] // blocks).reshape([-1 if axis == dim else 1 for axis in range(len(dims))])
    return loudness


def deal_out(key, own, number, rows, number_of, top, most, lean):
    ranking = jax.random.permutation(key, number_of)
    packed, usual = portions_of(number_of, rows * top, most, lean, True), portions_of(number_of, rows * top, most, lean, False)
    places = jnp.arange(number_of)

    def named(tallies, rotation):
        used = int((tallies > 0).sum())
        fixed = max(1, used // 4)
        moved = fixed + (places - fixed + rotation * (used - fixed)) % max(1, number_of - fixed)
        return jnp.zeros((number_of,), jnp.int32).at[ranking[jnp.where(places < fixed, places, moved)]].set(jnp.asarray(tallies, jnp.int32))

    tallies = jnp.where(number % 4 == 0, named(packed, number // 4), named(usual, number - number // 4 - 1))
    mixed = jax.random.permutation(jax.random.fold_in(own, 3), number_of)
    source_of, taker = mixed[0:number_of // 2 * 2:2], mixed[1:number_of // 2 * 2:2]
    slack = jnp.minimum(tallies[source_of] - 1, most - tallies[taker]) // 2
    slack = jnp.where((source_of == ranking[0]) | (taker == ranking[0]) | (tallies[taker] == 0), 0, jnp.maximum(slack, 0))
    moved = jax.random.randint(jax.random.fold_in(own, 4), (number_of // 2,), 0, 1 << 20) % (slack + 1)
    tallies = tallies.at[source_of].add(-moved).at[taker].add(moved)
    members = jnp.searchsorted(jnp.cumsum(tallies), jnp.arange(rows * top), side="right").astype(jnp.int32)
    grid = members.reshape(top, rows).T
    grid = grid[jax.random.permutation(jax.random.fold_in(own, 1), rows)]
    rotation = jax.random.randint(jax.random.fold_in(own, 2), (rows, 1), 0, top)
    return jnp.take_along_axis(grid, (jnp.arange(top)[None, :] + rotation) % top, axis=1)


def portions_of(count, total, reach, lean, full):
    weights = [(1 << 20) // math.isqrt(grade ** lean) + 1 for grade in range(1, count + 1)]
    largest = reach if full else min(reach, max(-(-total // count), total * weights[0] // sum(weights)))
    least = 1 if total - largest >= count - 1 else 0
    holding, rest = [largest] + [least] * (count - 1), total - largest - least * (count - 1)
    while rest > 0:
        free = [i for i in range(1, count) if holding[i] < largest] or [i for i in range(1, count) if holding[i] < reach]
        mass, budget = sum([weights[i] for i in free]), rest
        for i in free:
            addition = min(reach - holding[i], max(1, budget * weights[i] // mass), rest)
            holding[i] = holding[i] + addition
            rest = rest - addition
    return np.array(holding)


def setup_inputs(seed: int = 0) -> dict:
    keys = jax.random.split(jax.random.key(seed), 7)
    subvols = draw_subvols(jax.random.fold_in(keys[6], 71), 0)
    tomogram_keys = jax.random.split(jax.random.fold_in(keys[1], 1), SUBVOLS // SUB_DEV)
    tomogram_turns = jax.random.permutation(jax.random.fold_in(keys[1], 3), SUBVOLS // SUB_DEV)
    tomogram = jax.vmap(lambda own, number: deal_out(jax.random.fold_in(keys[1], 2), own, number, SUB_DEV, N_TILE, 1, CAPACITY, 2))(tomogram_keys, tomogram_turns).reshape((SUBVOLS, 1))
    sharpness = draw_sharpness(jax.random.fold_in(keys[6], 71), 0)
    references = draw_references(jax.random.fold_in(keys[6], 71), 0)
    interp = draw_interp(jax.random.fold_in(keys[6], 71), 0)
    weighting = jnp.clip(0.099609375 + 0.9003906 * jax.random.uniform(keys[5], (TOMOS, ORIENTS, VOXELS), jnp.float32) ** levels(keys[5], (TOMOS, ORIENTS, VOXELS), ((0, 32),), -0.2, 0.2), 0.099609375, 1.0).astype(jnp.bfloat16)
    return {"subvols": subvols, "tomogram": tomogram, "sharpness": sharpness, "references": references, "interp": interp, "weighting": weighting}


def rotate(volumes, interp):
    edge = interp.shape[-1]
    count = volumes.shape[0]
    matrices = interp.astype(jnp.float32)
    volume = volumes.astype(jnp.float32).reshape(count, edge, edge, edge)
    first_pass = jnp.einsum('rijl,ocl->orcij', volume, matrices[:, 2], precision=lax.Precision.HIGHEST).astype(jnp.bfloat16)
    second_pass = jnp.einsum('orcij,obj->orbci', first_pass.astype(jnp.float32), matrices[:, 1], precision=lax.Precision.HIGHEST).astype(jnp.bfloat16)
    third_pass = jnp.einsum('orbci,oai->orabc', second_pass.astype(jnp.float32), matrices[:, 0], precision=lax.Precision.HIGHEST).astype(jnp.bfloat16)
    return third_pass.reshape(interp.shape[0], count, edge ** 3)

def unrotate(volumes, interp):
    edge = interp.shape[-1]
    orients, count = (volumes.shape[0], volumes.shape[1])
    matrices = interp.astype(jnp.float32)
    volume = volumes.astype(jnp.float32).reshape(orients, count, edge, edge, edge)
    back_one = jnp.einsum('orabc,ocl->orlab', volume, matrices[:, 2], precision=lax.Precision.HIGHEST).astype(jnp.bfloat16)
    back_two = jnp.einsum('orlab,obj->orjla', back_one.astype(jnp.float32), matrices[:, 1], precision=lax.Precision.HIGHEST).astype(jnp.bfloat16)
    back_three = jnp.einsum('orjla,oai->orijl', back_two.astype(jnp.float32), matrices[:, 0], precision=lax.Precision.HIGHEST).astype(jnp.bfloat16)
    return back_three.reshape(orients, count, edge ** 3)

def normalize(summed):
    spread = jnp.sqrt(lax.optimization_barrier(jnp.mean(summed * summed, axis=1, keepdims=True)) + 1e-06)
    return (summed / spread).astype(jnp.bfloat16)

def slot_rows(tomogram):
    target = tomogram[:, 0].reshape(DEVICES, SUB_DEV)
    onehot = (target[:, :, None] == jnp.arange(N_TILE, dtype=jnp.int32)).astype(jnp.int32)
    within = lax.optimization_barrier(jnp.sum((jnp.cumsum(onehot, axis=1) - onehot) * onehot, axis=2))
    position = (target * CAPACITY + within).astype(jnp.int32)
    device_ids = jnp.broadcast_to(jnp.arange(DEVICES, dtype=jnp.int32)[:, None], (DEVICES, SUB_DEV))
    row_ids = jnp.arange(SUBVOLS, dtype=jnp.int32).reshape(DEVICES, SUB_DEV)
    send_rows = jnp.full((DEVICES, N_TILE * CAPACITY), SUBVOLS, jnp.int32).at[device_ids, position].set(row_ids)
    return send_rows.reshape(N_TILE, N_CLS, N_TILE, CAPACITY)

def reference(subvols, tomogram, sharpness, references, interp, weighting):
    send_rows = slot_rows(tomogram)
    current = references
    posterior = jnp.zeros((SUBVOLS, REFS), jnp.float32)
    for iteration in range(ITERS):
        rotated = rotate(current, interp)

        def group(summed, group_index):
            tile_index = group_index // N_CLS
            cls_index = group_index % N_CLS
            row_ids = send_rows[:, cls_index, tile_index, :].reshape(-1)
            received = jnp.take(subvols, row_ids, axis=0, mode='fill', fill_value=0)
            sharp_in = jnp.take(sharpness, row_ids, axis=0, mode='fill', fill_value=0)
            tomo_weight = weighting[tile_index].astype(jnp.float32)[:, None, :]
            filtered = (tomo_weight * rotated.astype(jnp.float32)).astype(jnp.bfloat16).reshape(ORIENTS * REFS, VOXELS)
            scale = sharp_in.astype(jnp.float32)[:, None] / math.sqrt(VOXELS)
            scores = jnp.dot(received, filtered.T, preferred_element_type=jnp.float32) * scale
            weights = jax.nn.softmax(scores, axis=1)
            weights_q = weights.astype(jnp.bfloat16)
            accum = jnp.dot(weights_q.T, received, preferred_element_type=jnp.float32).reshape(ORIENTS, REFS, VOXELS)
            accum = (accum * tomo_weight).astype(jnp.bfloat16)
            partial_value = lax.optimization_barrier(jnp.sum(unrotate(accum, interp).astype(jnp.float32), axis=0))
            class_prob = lax.optimization_barrier(jnp.sum(weights.reshape(-1, ORIENTS, REFS), axis=1))
            return (summed + partial_value, (class_prob, row_ids))
        summed, (class_probs, all_rows) = lax.scan(group, jnp.zeros((REFS, VOXELS), jnp.float32), jnp.arange(DEVICES, dtype=jnp.int32))
        current = normalize(summed)
        posterior = jnp.zeros((SUBVOLS, REFS), jnp.float32).at[all_rows.reshape(-1)].set(class_probs.reshape(-1, REFS), mode='drop')
    return (current, posterior)
```

```python
import math

import jax
import jax.numpy as jnp
from jax import lax
from jax.sharding import PartitionSpec as P

F32 = jnp.float32
BF = jnp.bfloat16


def shards(subvols, tomogram, sharpness, references, interp, weighting):
    count, voxels = subvols.shape
    orients, edge = interp.shape[0], interp.shape[-1]
    refs = lax.all_gather(references, "cls", axis=0, tiled=True)
    weight = lax.all_gather(weighting, "tile", axis=0, tiled=True)
    number = refs.shape[0]
    plane = edge * edge
    kron = jnp.einsum("obj,ocl->obcjl", interp[:, 1].astype(F32), interp[:, 2].astype(F32))
    kron = kron.astype(BF).reshape(orients, plane, plane)
    second = jnp.einsum(
        "rip,oqp->oriq", refs.reshape(number, edge, plane), kron, preferred_element_type=F32
    ).astype(BF)
    rotated = jnp.einsum("oriq,oai->oraq", second, interp[:, 0], preferred_element_type=F32)
    rotated = rotated.astype(BF).reshape(orients, number, voxels)
    own = jnp.take(weight, tomogram[:, 0], axis=0)
    weighted = (subvols.astype(F32)[:, None, :] * own.astype(F32)).astype(BF)
    scores = jnp.einsum("sov,orv->sor", weighted, rotated, preferred_element_type=F32)
    scores = scores * (sharpness.astype(F32) / math.sqrt(voxels))[:, None, None]
    weights = jax.nn.softmax(scores.reshape(count, -1), axis=1).reshape(scores.shape)
    posterior = jnp.sum(weights, axis=1)
    acc = jnp.einsum("sor,sov->orv", weights.astype(BF), weighted, preferred_element_type=F32)
    acc = acc.astype(BF).reshape(orients, number, edge, plane)
    back = jnp.einsum("oraq,oai->oriq", acc, interp[:, 0], preferred_element_type=F32).astype(BF)
    summed = jnp.einsum("oriq,oqp->rip", back, kron, preferred_element_type=F32)
    summed = summed.reshape(number, voxels).astype(BF)
    own_sum = lax.psum_scatter(summed, "cls", scatter_dimension=0, tiled=True)
    own_sum = lax.psum(own_sum, "tile").astype(F32)
    spread = jnp.sqrt(jnp.mean(own_sum * own_sum, axis=1, keepdims=True) + 1e-06)
    return (own_sum / spread).astype(BF), posterior


def solution(mesh):
    in_specs = (
        P(("tile", "cls"), None),
        P(("tile", "cls"), None),
        P(("tile", "cls")),
        P("cls", None),
        P(),
        P("tile", None, None),
    )
    out_specs = (P("cls", None), P(("tile", "cls"), None))
    return jax.shard_map(shards, mesh=mesh, in_specs=in_specs, out_specs=out_specs, check_vma=False)
```

```python
import functools
import math

import jax
import jax.numpy as jnp
from jax import lax
from jax.experimental import pallas as pl
from jax.experimental.pallas import tpu as pltpu
from jax.sharding import PartitionSpec as P

F32 = jnp.float32
BF = jnp.bfloat16
MESH = pl.DeviceIdType.MESH
EDGE = 32
PLANE = EDGE * EDGE
SIDE = 4
TILES = 32
DEPTH = 8
ORIENTS = 4
REFS = 8
ROWS = 32
CHUNKS = 8
PAIRS = CHUNKS // 2
NT = (((1,), (1,)), ((), ()))


def dot(a, b):
    return jnp.dot(a, b, preferred_element_type=F32)


def dot_nt(a, b):
    return lax.dot_general(a, b, NT, preferred_element_type=F32)


def iota(shape, dim):
    return lax.broadcasted_iota(jnp.int32, shape, dim)


def mask(cond):
    return jnp.where(cond, 1.0, 0.0).astype(BF)


def kernel(
    x_ref, tom_ref, sharp_ref, own_ref, interp_ref, w_ref,
    upd_ref, post_ref,
    wall, kron, cur, second, rot, y, pick, rep, fwd, bwd, sc, acc, back, total,
    out_s, in_s, out_z, in_z, full,
    ws, wr, rs, rr, ps, pr, zs, zr, fs, fr,
):
    tile, z = lax.axis_index("tile"), lax.axis_index("cls")
    core, xx, yy = tile % 2, (tile // 2) % SIDE, tile // (2 * SIDE)

    def at(y_, x_, c_):
        return ((y_ * SIDE + x_) * 2 + c_, z)

    sibling = (tile + 1 - 2 * core, z)

    def peer(d):
        return ((tile + d) % TILES, z)

    def above(d):
        return (tile, (z + d) % DEPTH)

    def remote(src, dst, ssem, rsem, dev):
        return pltpu.make_async_remote_copy(
            src_ref=src, dst_ref=dst, send_sem=ssem, recv_sem=rsem, device_id=dev, device_id_type=MESH
        )

    wall[:, yy, xx, core] = w_ref[...]
    cur[z] = own_ref[...]

    barrier = pltpu.get_barrier_semaphore()

    @pl.loop(1, TILES)
    def _(d):
        pl.semaphore_signal(barrier, inc=1, device_id=peer(d), device_id_type=MESH)

    @pl.loop(1, DEPTH)
    def _(d):
        pl.semaphore_signal(barrier, inc=1, device_id=above(d), device_id_type=MESH)

    pl.semaphore_wait(barrier, TILES - 1 + DEPTH - 1)

    half = pl.ds(pl.multiple_of(core * 16, 16), 16)

    def ref_copy(d):
        return remote(cur.at[z, half], cur.at[z, half], rs.at[d], rr.at[d], above(d))

    def ref_swap():
        return remote(cur.at[:, half], cur.at[:, half], rs.at[0], rr.at[0], sibling)

    @pl.loop(1, DEPTH)
    def _(d):
        ref_copy(d).start()

    def step(ch, sign, xfirst, kind):
        if kind == 6:
            block = wall.at[ch, :, :, core]
            dev = sibling
        else:
            leg = kind // 3
            along_x = xfirst == (leg == 0)
            hop = (1, -1, sign)[kind % 3]
            fwd_from = 0 if kind % 3 < 2 else -hop
            px = (xx + fwd_from + SIDE) % SIDE if along_x else xx
            py = yy if along_x else (yy + fwd_from + SIDE) % SIDE
            dev = at(yy, (xx + hop + SIDE) % SIDE, core) if along_x else at((yy + hop + SIDE) % SIDE, xx, core)
            if leg == 0:
                block = wall.at[ch, py, px, core]
            elif along_x:
                block = wall.at[ch, :, px, core]
            else:
                block = wall.at[ch, py, :, core]
        return remote(block, block, ws.at[ch, kind], wr.at[ch, kind], dev)

    def go(j, kinds):
        for kind in kinds:
            step(2 * j, 1 - 2 * (j % 2), True, kind).start()
            step(2 * j + 1, 1 - 2 * (j % 2), False, kind).start()

    def landed(j, kinds):
        for kind in kinds:
            step(2 * j, 1 - 2 * (j % 2), True, kind).wait_recv()
            step(2 * j + 1, 1 - 2 * (j % 2), False, kind).wait_recv()

    for j in range(PAIRS):
        go(j, (0, 1))

    def comm(j):
        if 0 <= j < PAIRS:
            landed(j, (0, 1))
            go(j, (2,))
        if 0 <= j - 1 < PAIRS:
            landed(j - 1, (2,))
            go(j - 1, (3, 4))
        if 0 <= j - 2 < PAIRS:
            landed(j - 2, (3, 4))
            go(j - 2, (5,))
        if 0 <= j - 3 < PAIRS:
            landed(j - 3, (5,))
            go(j - 3, (6,))

    def build(o):
        a1 = dot(interp_ref[o, 1], mask(iota((EDGE, PLANE), 1) // EDGE == iota((EDGE, PLANE), 0)))
        a2 = dot(interp_ref[o, 2], mask(iota((EDGE, PLANE), 1) % EDGE == iota((EDGE, PLANE), 0)))
        rep[...] = a1

        @pl.loop(0, EDGE)
        def _(b):
            kron[o, pl.ds(pl.multiple_of(b * EDGE, EDGE), EDGE), :] = (rep[pl.ds(b, 1), :] * a2).astype(BF)

        a0 = interp_ref[o, 0]
        select = mask(iota((256, EDGE), 0) // REFS == iota((256, EDGE), 1))
        row, col = iota((256, 256), 0), iota((256, 256), 1)
        spread = mask(iota((EDGE, 256), 1) % EDGE == iota((EDGE, 256), 0))
        wide = dot(dot(select, a0).astype(BF), spread)
        fwd[o] = jnp.where(row % REFS == col // EDGE, wide, 0.0).astype(BF)
        spread = mask(iota((EDGE, 256), 1) // REFS == iota((EDGE, 256), 0))
        wide = dot(dot_nt(select, a0).astype(BF), spread)
        bwd[o] = jnp.where(row % REFS == col % REFS, wide, 0.0).astype(BF)

    def rotate(o):
        flat = cur[...].reshape(256, PLANE)

        @pl.loop(0, 4)
        def _(n):
            cols = pl.ds(pl.multiple_of(n * 256, 256), 256)
            part = dot_nt(flat, kron[o, cols, :]).astype(BF)
            rot[:, o, :, cols] = dot(fwd[o], part).reshape(EDGE, REFS, 256)

    def score(ch):
        @pl.loop(0, 4)
        def _(n):
            cols = pl.ds(pl.multiple_of(n * 256, 256), 256)
            got = dot(pick[...], wall[ch, :, :, :, :, cols].reshape(512, 256))
            for sub in range(4):
                start = pl.multiple_of((ch * 4 + sub) * PLANE + n * 256, 256)
                rows = x_ref[:, pl.ds(start, 256)].astype(F32)
                prod = got[sub * 128 : sub * 128 + 128].reshape(ORIENTS, ROWS, 256) * rows[None]
                y[ch * 4 + sub, :, cols] = prod.reshape(128, 256).astype(BF)

        @pl.loop(0, 4)
        def _(sub):
            a = ch * 4 + sub
            sc[...] += dot_nt(rot[a].reshape(32, PLANE).astype(BF), y[a])

    sc[...] = jnp.zeros_like(sc)
    for sub in range(4):
        for o in range(ORIENTS):
            code = tom_ref[...] * 16 + (o * 4 + sub)
            pick[pl.ds((sub * 4 + o) * ROWS, ROWS), :] = mask(code == iota((ROWS, 512), 1))

    build(0)
    comm(0)
    build(1)
    comm(1)
    build(2)
    build(3)

    @pl.loop(1, DEPTH)
    def _(d):
        ref_copy(d).wait_recv()

    ref_swap().start()
    comm(2)
    ref_swap().wait_recv()
    pl.loop(0, 2)(rotate)
    comm(3)
    pl.loop(2, 4)(rotate)
    for j in range(4, 8):
        comm(j)
        landed(j - 4, (6,))
        pl.loop(2 * (j - 4), 2 * (j - 4) + 2)(score)

    raw = sc[...]
    pair = iota((32, 128), 0) // REFS
    lane = iota((32, 128), 1) // ROWS
    raw = jnp.where(pair == lane, raw, 0.0)
    scores = raw[:, 0:32] + raw[:, 32:64] + raw[:, 64:96] + raw[:, 96:128]
    scores = scores * sharp_ref[...]
    top = jnp.max(scores, axis=0, keepdims=True)
    expo = jnp.exp(scores - top)
    weights = expo / jnp.sum(expo, axis=0, keepdims=True)
    post_ref[...] = weights[0:8] + weights[8:16] + weights[16:24] + weights[24:32]
    tiled = jnp.concatenate([weights] * 4, axis=1)
    mixed = jnp.where(pair == lane, tiled, 0.0).astype(BF)

    @pl.loop(0, EDGE)
    def _(a):
        acc[:, a] = dot(mixed, y[a]).reshape(ORIENTS, REFS, PLANE)

    @pl.loop(0, ORIENTS)
    def _(o):
        cols = pl.ds(pl.multiple_of(o * PLANE, PLANE), PLANE)
        back[:, cols] = dot(bwd[o], acc[o].reshape(256, PLANE).astype(BF)).astype(BF)

    @pl.loop(0, 4)
    def _(n):
        cols = pl.ds(pl.multiple_of(n * 256, 256), 256)
        total[:, cols] = dot(back[...], kron[:, :, cols].reshape(ORIENTS * PLANE, 256))

    @pl.loop(0, EDGE)
    def _(i):
        part = total[pl.ds(pl.multiple_of(i * REFS, REFS), REFS), :]
        out_s[i] = jnp.concatenate([part[:, :512], part[:, 512:]], axis=0).astype(BF)

    def part_copy(d):
        dev = peer(d)
        return remote(out_s.at[dev[0]], in_s.at[d], ps.at[d], pr.at[d], dev)

    @pl.loop(1, TILES)
    def _(d):
        part_copy(d).start()

    @pl.loop(1, TILES)
    def _(d):
        part_copy(d).wait_recv()

    mine = lax.fori_loop(1, TILES, lambda d, s: s + in_s[d].astype(F32), out_s[tile].astype(F32))
    for block in range(8):
        rows, cols = (block // 4) * 8, (block % 4) * 128
        out_z[:, block, :] = mine[rows : rows + 8, cols : cols + 128]

    def z_copy(d):
        dev = above(d)
        return remote(out_z.at[dev[1]], in_z.at[d], zs.at[d], zr.at[d], dev)

    @pl.loop(1, DEPTH)
    def _(d):
        z_copy(d).start()

    @pl.loop(1, DEPTH)
    def _(d):
        z_copy(d).wait_recv()

    full[tile] = lax.fori_loop(1, DEPTH, lambda d, s: s + in_z[d], out_z[z])

    def full_copy(d):
        return remote(full.at[tile], full.at[tile], fs.at[d], fr.at[d], peer(d))

    @pl.loop(1, TILES)
    def _(d):
        full_copy(d).start()

    @pl.loop(1, DEPTH)
    def _(d):
        ref_copy(d).wait_send()
        z_copy(d).wait_send()

    ref_swap().wait_send()
    for j in range(PAIRS):
        for kind in range(7):
            step(2 * j, 1 - 2 * (j % 2), True, kind).wait_send()
            step(2 * j + 1, 1 - 2 * (j % 2), False, kind).wait_send()

    @pl.loop(1, TILES)
    def _(d):
        part_copy(d).wait_send()

    @pl.loop(1, TILES)
    def _(d):
        full_copy(d).wait_recv()

    whole = full[...].reshape(256, 128)
    mean = jnp.sum(whole * whole) / (EDGE * PLANE)
    upd_ref[...] = (whole / jnp.sqrt(mean + 1e-06)).astype(BF)

    @pl.loop(1, TILES)
    def _(d):
        full_copy(d).wait_send()


def shards(subvols, tomogram, sharpness, references, interp, weighting):
    rows, voxels = subvols.shape
    sharp = (sharpness.astype(F32) / math.sqrt(voxels)).reshape(1, rows)
    own = references.reshape(EDGE, PLANE)
    weight = weighting.reshape(ORIENTS, CHUNKS, 4, PLANE).transpose(1, 0, 2, 3).reshape(CHUNKS, 16, PLANE)
    vmem = pl.BlockSpec(memory_space=pltpu.VMEM)
    dma = pltpu.SemaphoreType.DMA
    updated, posterior = pl.pallas_call(
        kernel,
        out_shape=(
            jax.ShapeDtypeStruct((256, 128), BF),
            jax.ShapeDtypeStruct((REFS, rows), F32),
        ),
        in_specs=[vmem] * 6,
        out_specs=(vmem, vmem),
        scratch_shapes=[
            pltpu.VMEM((CHUNKS, SIDE, SIDE, 2, 16, PLANE), BF),
            pltpu.VMEM((ORIENTS, PLANE, PLANE), BF),
            pltpu.VMEM((REFS, EDGE, PLANE), BF),
            pltpu.VMEM((256, PLANE), BF),
            pltpu.VMEM((EDGE, ORIENTS, REFS, PLANE), F32),
            pltpu.VMEM((EDGE, ORIENTS * rows, PLANE), BF),
            pltpu.VMEM((512, 512), BF),
            pltpu.VMEM((EDGE, PLANE), F32),
            pltpu.VMEM((ORIENTS, 256, 256), BF),
            pltpu.VMEM((ORIENTS, 256, 256), BF),
            pltpu.VMEM((32, 128), F32),
            pltpu.VMEM((ORIENTS, EDGE, REFS, PLANE), F32),
            pltpu.VMEM((256, ORIENTS * PLANE), BF),
            pltpu.VMEM((256, PLANE), F32),
            pltpu.VMEM((TILES, 16, 512), BF),
            pltpu.VMEM((TILES, 16, 512), BF),
            pltpu.VMEM((REFS, 8, 128), F32),
            pltpu.VMEM((DEPTH, 8, 128), F32),
            pltpu.VMEM((TILES, 8, 128), F32),
            dma((CHUNKS, 7)),
            dma((CHUNKS, 7)),
            dma((DEPTH,)),
            dma((DEPTH,)),
            dma((TILES,)),
            dma((TILES,)),
            dma((DEPTH,)),
            dma((DEPTH,)),
            dma((TILES,)),
            dma((TILES,)),
        ],
        compiler_params=pltpu.CompilerParams(
            collective_id=0, has_side_effects=True, vmem_limit_bytes=56 * 1024 * 1024
        ),
    )(subvols, tomogram, sharp, own, interp, weight)
    return updated.reshape(1, voxels), posterior.T


def solution(mesh):
    in_specs = (
        P(("tile", "cls"), None),
        P(("tile", "cls"), None),
        P(("tile", "cls")),
        P("cls", None),
        P(),
        P("tile", None, None),
    )
    out_specs = (P("cls", None), P(("tile", "cls"), None))
    return jax.shard_map(shards, mesh=mesh, in_specs=in_specs, out_specs=out_specs, check_vma=False)
```

```python
import functools
import math

import jax
import jax.numpy as jnp
from jax import lax
from jax.experimental import pallas as pl
from jax.experimental.pallas import tpu as pltpu
from jax.sharding import PartitionSpec as P

F32 = jnp.float32
BF = jnp.bfloat16
MESH = pl.DeviceIdType.MESH
EDGE = 32
PLANE = EDGE * EDGE
SIDE = 4
TILES = 32
DEPTH = 8
ORIENTS = 4
REFS = 8
ROWS = 32
CHUNKS = 8
PAIRS = 3
NT = (((1,), (1,)), ((), ()))


def dot(a, b):
    return jnp.dot(a, b, preferred_element_type=F32)


def dot_nt(a, b):
    return lax.dot_general(a, b, NT, preferred_element_type=F32)


def iota(shape, dim):
    return lax.broadcasted_iota(jnp.int32, shape, dim)


def mask(cond):
    return jnp.where(cond, 1.0, 0.0).astype(BF)


def kernel(
    x_hbm, tom_hbm, sharp_hbm, own_hbm, interp_hbm, w_hbm,
    upd_ref, post_ref,
    x_ref, tom_ref, sharp_ref, own_ref, interp_ref, w_ref,
    wall, kron, cur, stage, rot, y, pick, rep, fwd, bwd, sc, acc, back,
    out_s, near, both, in_s, out_z, in_z, full, flat,
    ls, ws, wr, rs, rr, qs, qr, ps, pr, zs, zr, fs, fr,
):
    places = (x_ref, tom_ref, sharp_ref, own_ref, interp_ref, w_ref)
    loads = [
        pltpu.make_async_copy(source, place, ls.at[n])
        for n, (source, place) in enumerate(zip((x_hbm, tom_hbm, sharp_hbm, own_hbm, interp_hbm, w_hbm), places))
    ]
    for n in (5, 3, 4, 1, 2, 0):
        loads[n].start()

    tile, z = lax.axis_index("tile"), lax.axis_index("cls")
    core, xx, yy = tile % 2, (tile // 2) % SIDE, tile // (2 * SIDE)

    def at(y_, x_, c_):
        return ((y_ * SIDE + x_) * 2 + c_, z)

    sibling = (tile + 1 - 2 * core, z)

    def peer(d):
        return ((tile + d) % TILES, z)

    def above(d):
        return (tile, (z + d) % DEPTH)

    def remote(src, dst, ssem, rsem, dev):
        return pltpu.make_async_remote_copy(
            src_ref=src, dst_ref=dst, send_sem=ssem, recv_sem=rsem, device_id=dev, device_id_type=MESH
        )

    barrier = pltpu.get_barrier_semaphore()

    @pl.loop(1, TILES)
    def _(d):
        pl.semaphore_signal(barrier, inc=1, device_id=peer(d), device_id_type=MESH)

    @pl.loop(1, DEPTH)
    def _(d):
        pl.semaphore_signal(barrier, inc=1, device_id=above(d), device_id_type=MESH)

    loads[3].wait()
    loads[5].wait()
    for a in range(EDGE):
        cols = slice(a * PLANE, (a + 1) * PLANE)
        stage[a // 4, (a % 4) * 4 : (a % 4) * 4 + 4, :] = w_ref[0, :, cols].astype(F32)
        rep[a : a + 1, :] = own_ref[:, cols].astype(F32)
    mine_first = pl.ds(2 - 2 * (z % 2), 2)
    wall[mine_first, 0, 0, core] = stage[mine_first].astype(BF)
    wall[4:, 0, 0, core] = stage[4:].astype(BF)
    half = pl.ds(pl.multiple_of(core * 16, 16), 16)
    cur[z, half] = rep[half, :].astype(BF)

    pl.semaphore_wait(barrier, TILES - 1 + DEPTH - 1)

    def ref_copy(d):
        return remote(cur.at[z, half], cur.at[z, half], rs.at[d], rr.at[d], above(d))

    def ref_swap():
        return remote(cur.at[:, half], cur.at[:, half], rs.at[0], rr.at[0], sibling)

    ours, theirs = 2 - 2 * (z % 2), 2 * (z % 2)
    HOPS, LANDS = (1, -1, 2), (3, 1, 2)

    def chunk(j, xfirst):
        start = (ours, 4, 6, theirs)[j]
        return start if xfirst else start + 1

    def step(j, xfirst, kind):
        ch = chunk(j, xfirst)

        def block(line, place):
            return wall.at[ch, line, place, core] if xfirst else wall.at[ch, place, line, core]

        def along(first, hop):
            if first == xfirst:
                return at(yy, (xx + hop + SIDE) % SIDE, core)
            return at((yy + hop + SIDE) % SIDE, xx, core)

        rest = pl.ds(1, 3)
        if kind < 3:
            source, target, dev = block(0, 0), block(0, LANDS[kind]), along(True, HOPS[kind])
        elif kind < 6:
            source, target, dev = block(0, 0), block(LANDS[kind - 3], 0), along(False, HOPS[kind - 3])
        elif kind == 8 and j < PAIRS - 1:
            sign = 1 - 2 * (j % 2)
            source, target, dev = block(2 + sign, rest), block(2, rest), along(False, sign)
        elif kind < 9:
            source, target, dev = block(0, rest), block(LANDS[kind - 6], rest), along(False, HOPS[kind - 6])
        else:
            source = target = block((0, 3, 1, 2)[(kind - 9) % 4], pl.ds(0, 4))
            dev = sibling if kind < 13 else above(1 if xfirst else DEPTH - 1)
        return remote(source, target, ws.at[ch, kind], wr.at[ch, kind], dev)

    def go(j, kinds):
        for kind in kinds:
            step(j, True, kind).start()
            step(j, False, kind).start()

    def landed(j, kinds):
        for kind in kinds:
            step(j, True, kind).wait_recv()
            step(j, False, kind).wait_recv()

    def second(j):
        landed(j, (0, 1, 2))
        go(j, ((13, 6, 7, 9), (6, 7, 9), (6, 7, 8, 9))[j])

    def third(j):
        landed(j, (3, 4, 6, 7))
        go(j, ((8, 14, 15, 10, 11), (8, 10, 11), (10, 11))[j])

    def fourth(j):
        landed(j, (5, 8))
        go(j, ((16, 12), (12,), (12,))[j])

    def beside(*lines):
        for line in lines:
            landed(3, (13 + line,))
            go(3, (9 + line,))

    def build(o):
        a1 = dot(interp_ref[o, 1], mask(iota((EDGE, PLANE), 1) // EDGE == iota((EDGE, PLANE), 0)))
        a2 = dot(interp_ref[o, 2], mask(iota((EDGE, PLANE), 1) % EDGE == iota((EDGE, PLANE), 0)))
        rep[...] = a1

        @pl.loop(0, EDGE)
        def _(b):
            kron[o, pl.ds(pl.multiple_of(b * EDGE, EDGE), EDGE), :] = (rep[pl.ds(b, 1), :] * a2).astype(BF)

        a0 = interp_ref[o, 0]
        select = mask(iota((256, EDGE), 0) // REFS == iota((256, EDGE), 1))
        row, col = iota((256, 256), 0), iota((256, 256), 1)
        spread = mask(iota((EDGE, 256), 1) % EDGE == iota((EDGE, 256), 0))
        wide = dot(dot(select, a0).astype(BF), spread)
        fwd[o] = jnp.where(row % REFS == col // EDGE, wide, 0.0).astype(BF)
        spread = mask(iota((EDGE, 256), 1) // REFS == iota((EDGE, 256), 0))
        wide = dot(dot_nt(select, a0).astype(BF), spread)
        bwd[o] = jnp.where(row % REFS == col % REFS, wide, 0.0).astype(BF)

    def rotate(o):
        volumes = cur[...].reshape(256, PLANE)
        for n in range(4):
            cols = slice(n * 256, (n + 1) * 256)
            part = dot_nt(volumes, kron[o, cols, :]).astype(BF)
            got = dot(fwd[o], part).reshape(CHUNKS, 4, REFS, 256)
            for sub in range(4):
                spot = slice(sub * PLANE + n * 256, sub * PLANE + (n + 1) * 256)
                rot[:, pl.ds(pl.multiple_of(o * REFS, REFS), REFS), spot] = got[:, sub]

    def weigh(ch):
        for h in range(2):
            for n in range(4):
                cols = slice(n * 256, (n + 1) * 256)
                got = dot(pick[...], wall[ch, :, :, :, h * 8 : h * 8 + 8, cols].reshape(256, 256))
                for sub in range(2):
                    spot = (h * 2 + sub) * PLANE + n * 256
                    rows = x_ref[:, pl.ds(pl.multiple_of(ch * 4 * PLANE + spot, 256), 256)].astype(F32)
                    prod = got[sub * 128 : sub * 128 + 128].reshape(ORIENTS, ROWS, 256) * rows[None]
                    y[ch, :, spot : spot + 256] = prod.reshape(128, 256).astype(BF)

    def fifth(j):
        landed(j, (9, 10, 11, 12))
        start = chunk(j, True)
        pl.loop(start, start + 2)(weigh)

    def score(ch):
        sc[...] += dot_nt(y[ch], rot[ch].astype(BF))

    go(0, (0, 1, 2, 3, 4, 5))
    go(1, (0, 1, 2))

    @pl.loop(1, DEPTH)
    def _(d):
        ref_copy(d).start()

    loads[4].wait()
    pl.loop(0, 2)(build)
    second(0)
    go(1, (3, 4, 5))
    go(2, (0, 1, 2))
    pl.loop(2, 4)(build)
    second(1)
    loads[1].wait()
    loads[2].wait()
    sc[...] = jnp.zeros_like(sc)
    diagonal = iota((ROWS, ROWS), 0) == iota((ROWS, ROWS), 1)
    named = jnp.sum(jnp.where(diagonal, tom_ref[...].astype(F32), 0.0), axis=1, keepdims=True).astype(jnp.int32)
    away_y = (named // (2 * SIDE) + SIDE - yy) % SIDE
    away_x = (named // 2 + SIDE - xx) % SIDE
    named = (away_y * SIDE + away_x) * 2 + named % 2
    for sub in range(2):
        for o in range(ORIENTS):
            code = named * 8 + (sub * 4 + o)
            pick[pl.ds((sub * 4 + o) * ROWS, ROWS), :] = mask(code == iota((ROWS, 256), 1))
    third(0)
    go(2, (3, 4, 5))
    second(2)

    @pl.loop(1, DEPTH)
    def _(d):
        ref_copy(d).wait_recv()

    ref_swap().start()
    fourth(0)
    third(1)
    ref_swap().wait_recv()
    pl.loop(0, 1)(rotate)
    third(2)
    fourth(1)
    beside(0)
    pl.loop(1, 2)(rotate)
    beside(1)
    fourth(2)
    pl.loop(2, 3)(rotate)
    beside(2, 3)
    loads[0].wait()
    fifth(0)
    pl.loop(3, 4)(rotate)
    fifth(1)
    fifth(2)
    pl.loop(4, 8)(score)
    fifth(3)
    pl.loop(0, 4)(score)

    raw = jnp.concatenate([sc[...], jnp.zeros((128, 96), F32)], axis=1).T[:32]
    pair = iota((32, 128), 0) // REFS
    lane = iota((32, 128), 1) // ROWS
    raw = jnp.where(pair == lane, raw, 0.0)
    scores = raw[:, 0:32] + raw[:, 32:64] + raw[:, 64:96] + raw[:, 96:128]
    scores = scores * (sharp_ref[...].astype(F32) * (1 / math.sqrt(EDGE * PLANE)))
    top = jnp.max(scores, axis=0, keepdims=True)
    expo = jnp.exp(scores - top)
    weights = expo / jnp.sum(expo, axis=0, keepdims=True)
    post_ref[...] = weights[0:8] + weights[8:16] + weights[16:24] + weights[24:32]
    tiled = jnp.concatenate([weights] * 4, axis=1)
    mixed = jnp.where(pair == lane, tiled, 0.0).astype(BF)

    @pl.loop(0, CHUNKS)
    def _(ch):
        got = dot(mixed, y[ch])
        for sub in range(4):
            acc[:, ch * 4 + sub] = got[:, sub * PLANE : (sub + 1) * PLANE].reshape(ORIENTS, REFS, PLANE)

    for o in range(ORIENTS):
        back[:, o * PLANE : (o + 1) * PLANE] = dot(bwd[o], acc[o].reshape(256, PLANE).astype(BF)).astype(BF)

    def owner(n, k):
        return (k * SIDE + (n + k) % SIDE) * 2 + core

    def pair_copy(n):
        return remote(out_s.at[n, 1 - core], near.at[n], qs.at[n], qr.at[n], sibling)

    def part_copy(n, k):
        chip = tile // 2
        return remote(both.at[n, k], in_s.at[chip], ps.at[n, k], pr.at[chip], (owner(n, k), z))

    def part_arrival(d):
        chip = (tile // 2 + d) % (TILES // 2)
        return remote(in_s.at[chip], in_s.at[chip], ps.at[0, 0], pr.at[chip], (tile, z))

    def send_parts(n):
        pair_copy(n).wait_recv()
        both[n] = (out_s[n, core].astype(F32) + near[n].astype(F32)).astype(BF)

        @pl.loop(0, SIDE)
        def _(k):
            @pl.when(owner(n, k) != tile)
            def _():
                part_copy(n, k).start()

    for n in range(4):
        got = dot(back[...], kron[:, :, n * 256 : (n + 1) * 256].reshape(ORIENTS * PLANE, 256)).astype(BF)
        for k in range(8):
            out_s[n, k % 2, k // 2] = got[k * 32 : k * 32 + 32]
        pair_copy(n).start()
        if n:
            send_parts(n - 1)
    send_parts(3)

    @pl.loop(1, TILES // 2)
    def _(d):
        part_arrival(d).wait_recv()

    def add(d, so_far):
        return so_far + in_s[(tile // 2 + d) % (TILES // 2)].astype(F32)

    mine = lax.fori_loop(1, TILES // 2, add, both[(xx - yy + SIDE) % SIDE, yy].astype(F32))
    for block in range(8):
        rows, cols = (block // 2) * 8, (block % 2) * 128
        out_z[:, block, :] = mine[rows : rows + 8, cols : cols + 128]

    def z_copy(d):
        dev = above(d)
        return remote(out_z.at[dev[1]], in_z.at[d], zs.at[d], zr.at[d], dev)

    @pl.loop(1, DEPTH)
    def _(d):
        z_copy(d).start()

    @pl.loop(1, DEPTH)
    def _(d):
        z_copy(d).wait_recv()

    full[tile] = lax.fori_loop(1, DEPTH, lambda d, s: s + in_z[d], out_z[z])

    def full_copy(d):
        return remote(full.at[tile], full.at[tile], fs.at[d], fr.at[d], peer(d))

    @pl.loop(1, TILES)
    def _(d):
        full_copy(d).start()

    @pl.loop(1, DEPTH)
    def _(d):
        z_copy(d).wait_send()

    ref_swap().wait_send()

    @pl.loop(1, DEPTH)
    def _(d):
        ref_copy(d).wait_send()

    for j in range(4):
        for kind in (range(17), range(13), range(13), range(9, 13))[j]:
            step(j, True, kind).wait_send()
            step(j, False, kind).wait_send()

    for n in range(4):
        pair_copy(n).wait_send()

        @pl.loop(0, SIDE)
        def _(k):
            @pl.when(owner(n, k) != tile)
            def _():
                part_copy(n, k).wait_send()

    @pl.loop(1, TILES)
    def _(d):
        full_copy(d).wait_recv()

    whole = full[...].reshape(256, 128)
    mean = jnp.sum(whole * whole) / (EDGE * PLANE)
    scale = 1 / jnp.sqrt(mean + 1e-06)
    for n in range(4):
        for k in range(8):
            got = full[(k // 2 * SIDE + (n + k // 2) % SIDE) * 2 + k % 2]
            for i in range(4):
                spot = (k * 4 + i) * 8 + n * 2
                flat[spot : spot + 2, :] = got[i * 2 : i * 2 + 2]
    upd_ref[...] = (flat[...] * scale).astype(BF)

    @pl.loop(1, TILES)
    def _(d):
        full_copy(d).wait_send()


def shards(subvols, tomogram, sharpness, references, interp, weighting):
    rows, voxels = subvols.shape
    vmem = pl.BlockSpec(memory_space=pltpu.VMEM)
    dma = pltpu.SemaphoreType.DMA
    updated, posterior = pl.pallas_call(
        kernel,
        out_shape=(
            jax.ShapeDtypeStruct((256, 128), BF),
            jax.ShapeDtypeStruct((REFS, rows), F32),
        ),
        in_specs=[pl.BlockSpec(memory_space=pl.ANY)] * 6,
        out_specs=(vmem, vmem),
        scratch_shapes=[
            pltpu.VMEM((rows, voxels), BF),
            pltpu.VMEM((1, rows), jnp.int32),
            pltpu.VMEM((1, rows), BF),
            pltpu.VMEM((1, voxels), BF),
            pltpu.VMEM((ORIENTS, 3, EDGE, EDGE), BF),
            pltpu.VMEM((1, ORIENTS, voxels), BF),
            pltpu.VMEM((CHUNKS, SIDE, SIDE, 2, 16, PLANE), BF),
            pltpu.VMEM((ORIENTS, PLANE, PLANE), BF),
            pltpu.VMEM((REFS, EDGE, PLANE), BF),
            pltpu.VMEM((CHUNKS, 16, PLANE), F32),
            pltpu.VMEM((CHUNKS, ORIENTS * REFS, 4 * PLANE), F32),
            pltpu.VMEM((CHUNKS, ORIENTS * rows, 4 * PLANE), BF),
            pltpu.VMEM((256, 256), BF),
            pltpu.VMEM((EDGE, PLANE), F32),
            pltpu.VMEM((ORIENTS, 256, 256), BF),
            pltpu.VMEM((ORIENTS, 256, 256), BF),
            pltpu.VMEM((128, 32), F32),
            pltpu.VMEM((ORIENTS, EDGE, REFS, PLANE), F32),
            pltpu.VMEM((256, ORIENTS * PLANE), BF),
            pltpu.VMEM((4, 2, SIDE, 32, 256), BF),
            pltpu.VMEM((4, SIDE, 32, 256), BF),
            pltpu.VMEM((4, SIDE, 32, 256), BF),
            pltpu.VMEM((TILES // 2, 32, 256), BF),
            pltpu.VMEM((REFS, 8, 128), F32),
            pltpu.VMEM((DEPTH, 8, 128), F32),
            pltpu.VMEM((TILES, 8, 128), F32),
            pltpu.VMEM((256, 128), F32),
            dma((6,)),
            dma((CHUNKS, 17)),
            dma((CHUNKS, 17)),
            dma((DEPTH,)),
            dma((DEPTH,)),
            dma((4,)),
            dma((4,)),
            dma((4, SIDE)),
            dma((TILES // 2,)),
            dma((DEPTH,)),
            dma((DEPTH,)),
            dma((TILES,)),
            dma((TILES,)),
        ],
        compiler_params=pltpu.CompilerParams(
            collective_id=0, has_side_effects=True, vmem_limit_bytes=56 * 1024 * 1024
        ),
    )(subvols, tomogram.reshape(1, rows), sharpness.reshape(1, rows), references, interp, weighting)
    return updated.reshape(1, voxels), posterior.T


def solution(mesh):
    in_specs = (
        P(("tile", "cls"), None),
        P(("tile", "cls"), None),
        P(("tile", "cls")),
        P("cls", None),
        P(),
        P("tile", None, None),
    )
    out_specs = (P("cls", None), P(("tile", "cls"), None))
    return jax.shard_map(shards, mesh=mesh, in_specs=in_specs, out_specs=out_specs, check_vma=False)
```

```python
import functools
import math

import jax
import jax.numpy as jnp
from jax import lax
from jax.experimental import pallas as pl
from jax.experimental.pallas import tpu as pltpu
from jax.sharding import PartitionSpec as P

F32 = jnp.float32
BF = jnp.bfloat16
MESH = pl.DeviceIdType.MESH
EDGE = 32
PLANE = EDGE * EDGE
SIDE = 4
TILES = 32
DEPTH = 8
ORIENTS = 4
REFS = 8
ROWS = 32
CHUNKS = 8
PAIRS = 3
NT = (((1,), (1,)), ((), ()))


def dot(a, b):
    return jnp.dot(a, b, preferred_element_type=F32)


def dot_nt(a, b):
    return lax.dot_general(a, b, NT, preferred_element_type=F32)


def iota(shape, dim):
    return lax.broadcasted_iota(jnp.int32, shape, dim)


def mask(cond):
    return jnp.where(cond, 1.0, 0.0).astype(BF)


def kernel(
    x_hbm, tom_hbm, sharp_hbm, own_hbm, interp_hbm, w_hbm,
    upd_ref, post_ref,
    x_ref, tom_ref, sharp_ref, own_ref, interp_ref, w_ref,
    wall, kron, cur, stage, rot, y, pick, rep, fwd, bwd, sc, acc, back,
    out_s, near, both, in_s, out_z, in_z, full, flat,
    ls, ws, wr, rs, rr, qs, qr, ps, pr, zs, zr, fs, fr,
):
    places = (x_ref, tom_ref, sharp_ref, own_ref, interp_ref, w_ref)
    loads = [
        pltpu.make_async_copy(source, place, ls.at[n])
        for n, (source, place) in enumerate(zip((x_hbm, tom_hbm, sharp_hbm, own_hbm, interp_hbm, w_hbm), places))
    ]
    for n in (5, 3, 4, 1, 2, 0):
        loads[n].start()

    tile, z = lax.axis_index("tile"), lax.axis_index("cls")
    core, xx, yy = tile % 2, (tile // 2) % SIDE, tile // (2 * SIDE)

    def at(y_, x_, c_):
        return ((y_ * SIDE + x_) * 2 + c_, z)

    sibling = (tile + 1 - 2 * core, z)

    def peer(d):
        return ((tile + d) % TILES, z)

    def above(d):
        return (tile, (z + d) % DEPTH)

    def remote(src, dst, ssem, rsem, dev):
        return pltpu.make_async_remote_copy(
            src_ref=src, dst_ref=dst, send_sem=ssem, recv_sem=rsem, device_id=dev, device_id_type=MESH
        )

    barrier = pltpu.get_barrier_semaphore()

    @pl.loop(1, TILES)
    def _(d):
        pl.semaphore_signal(barrier, inc=1, device_id=peer(d), device_id_type=MESH)

    @pl.loop(1, DEPTH)
    def _(d):
        pl.semaphore_signal(barrier, inc=1, device_id=above(d), device_id_type=MESH)

    loads[3].wait()
    loads[5].wait()
    for a in range(EDGE):
        cols = slice(a * PLANE, (a + 1) * PLANE)
        stage[a // 4, (a % 4) * 4 : (a % 4) * 4 + 4, :] = w_ref[0, :, cols].astype(F32)
        rep[a : a + 1, :] = own_ref[:, cols].astype(F32)
    mine_first = pl.ds(2 - 2 * (z % 2), 2)
    wall[mine_first, 0, 0, core] = stage[mine_first].astype(BF)
    wall[4:, 0, 0, core] = stage[4:].astype(BF)
    half = pl.ds(pl.multiple_of(core * 16, 16), 16)
    cur[z, half] = rep[half, :].astype(BF)

    pl.semaphore_wait(barrier, TILES - 1 + DEPTH - 1)

    def ref_copy(d):
        return remote(cur.at[z, half], cur.at[z, half], rs.at[d], rr.at[d], above(d))

    def ref_swap():
        return remote(cur.at[:, half], cur.at[:, half], rs.at[0], rr.at[0], sibling)

    ours, theirs = 2 - 2 * (z % 2), 2 * (z % 2)
    HOPS, LANDS = (1, -1, 2), (3, 1, 2)

    def chunk(j, xfirst):
        start = (ours, 4, 6, theirs)[j]
        return start if xfirst else start + 1

    def step(j, xfirst, kind):
        ch = chunk(j, xfirst)

        def block(line, place):
            return wall.at[ch, line, place, core] if xfirst else wall.at[ch, place, line, core]

        def along(first, hop):
            if first == xfirst:
                return at(yy, (xx + hop + SIDE) % SIDE, core)
            return at((yy + hop + SIDE) % SIDE, xx, core)

        rest = pl.ds(1, 3)
        if kind < 3:
            source, target, dev = block(0, 0), block(0, LANDS[kind]), along(True, HOPS[kind])
        elif kind < 6:
            source, target, dev = block(0, 0), block(LANDS[kind - 3], 0), along(False, HOPS[kind - 3])
        elif kind == 8 and j < PAIRS - 1:
            sign = 1 - 2 * (j % 2)
            source, target, dev = block(2 + sign, rest), block(2, rest), along(False, sign)
        elif kind < 9:
            source, target, dev = block(0, rest), block(LANDS[kind - 6], rest), along(False, HOPS[kind - 6])
        else:
            source = target = block((0, 3, 1, 2)[(kind - 9) % 4], pl.ds(0, 4))
            dev = sibling if kind < 13 else above(1 if xfirst else DEPTH - 1)
        return remote(source, target, ws.at[ch, kind], wr.at[ch, kind], dev)

    def go(j, kinds):
        for kind in kinds:
            step(j, True, kind).start()
            step(j, False, kind).start()

    def landed(j, kinds):
        for kind in kinds:
            step(j, True, kind).wait_recv()
            step(j, False, kind).wait_recv()

    def second(j):
        landed(j, (0, 1, 2))
        go(j, ((13, 6, 7, 9), (6, 7, 9), (6, 7, 8, 9))[j])

    def third(j):
        landed(j, (3, 4, 6, 7))
        go(j, ((8, 14, 15, 10, 11), (8, 10, 11), (10, 11))[j])

    def fourth(j):
        landed(j, (5, 8))
        go(j, ((16, 12), (12,), (12,))[j])

    def beside(*lines):
        for line in lines:
            landed(3, (13 + line,))
            go(3, (9 + line,))

    def build(o):
        a1 = dot(interp_ref[o, 1], mask(iota((EDGE, PLANE), 1) // EDGE == iota((EDGE, PLANE), 0)))
        a2 = dot(interp_ref[o, 2], mask(iota((EDGE, PLANE), 1) % EDGE == iota((EDGE, PLANE), 0)))
        rep[...] = a1

        @pl.loop(0, EDGE)
        def _(b):
            kron[o, pl.ds(pl.multiple_of(b * EDGE, EDGE), EDGE), :] = (rep[pl.ds(b, 1), :] * a2).astype(BF)

        a0 = interp_ref[o, 0]
        select = mask(iota((256, EDGE), 0) // REFS == iota((256, EDGE), 1))
        row, col = iota((256, 256), 0), iota((256, 256), 1)
        spread = mask(iota((EDGE, 256), 1) % EDGE == iota((EDGE, 256), 0))
        wide = dot(dot(select, a0).astype(BF), spread)
        fwd[o] = jnp.where(row % REFS == col // EDGE, wide, 0.0).astype(BF)
        spread = mask(iota((EDGE, 256), 1) // REFS == iota((EDGE, 256), 0))
        wide = dot(dot_nt(select, a0).astype(BF), spread)
        bwd[o] = jnp.where(row % REFS == col % REFS, wide, 0.0).astype(BF)

    def rotate(o):
        volumes = cur[...].reshape(256, PLANE)
        for n in range(4):
            cols = slice(n * 256, (n + 1) * 256)
            part = dot_nt(volumes, kron[o, cols, :]).astype(BF)
            got = dot(fwd[o], part).reshape(CHUNKS, 4, REFS, 256)
            for sub in range(4):
                spot = slice(sub * PLANE + n * 256, sub * PLANE + (n + 1) * 256)
                rot[:, pl.ds(pl.multiple_of(o * REFS, REFS), REFS), spot] = got[:, sub]

    def weigh(ch):
        for h in range(2):
            for n in range(4):
                cols = slice(n * 256, (n + 1) * 256)
                got = dot(pick[...], wall[ch, :, :, :, h * 8 : h * 8 + 8, cols].reshape(256, 256))
                for sub in range(2):
                    spot = (h * 2 + sub) * PLANE + n * 256
                    rows = x_ref[:, pl.ds(pl.multiple_of(ch * 4 * PLANE + spot, 256), 256)].astype(F32)
                    prod = got[sub * 128 : sub * 128 + 128].reshape(ORIENTS, ROWS, 256) * rows[None]
                    y[ch, :, spot : spot + 256] = prod.reshape(128, 256).astype(BF)

    def score(ch):
        sc[...] += dot_nt(y[ch], rot[ch].astype(BF))

    go(0, (0, 1, 2, 3, 4, 5))
    go(1, (0, 1, 2))

    @pl.loop(1, DEPTH)
    def _(d):
        ref_copy(d).start()

    loads[4].wait()

    @pl.loop(0, ORIENTS)
    def _(o):
        build(o)

        @pl.when(o == 1)
        def _():
            second(0)
            go(1, (3, 4, 5))
            go(2, (0, 1, 2))

    second(1)
    loads[1].wait()
    loads[2].wait()
    sc[...] = jnp.zeros_like(sc)
    diagonal = iota((ROWS, ROWS), 0) == iota((ROWS, ROWS), 1)
    named = jnp.sum(jnp.where(diagonal, tom_ref[...].astype(F32), 0.0), axis=1, keepdims=True).astype(jnp.int32)
    away_y = (named // (2 * SIDE) + SIDE - yy) % SIDE
    away_x = (named // 2 + SIDE - xx) % SIDE
    named = (away_y * SIDE + away_x) * 2 + named % 2
    for sub in range(2):
        for o in range(ORIENTS):
            code = named * 8 + (sub * 4 + o)
            pick[pl.ds((sub * 4 + o) * ROWS, ROWS), :] = mask(code == iota((ROWS, 256), 1))
    third(0)
    go(2, (3, 4, 5))
    second(2)

    @pl.loop(1, DEPTH)
    def _(d):
        ref_copy(d).wait_recv()

    ref_swap().start()
    fourth(0)
    third(1)
    ref_swap().wait_recv()

    @pl.loop(0, ORIENTS)
    def _(o):
        rotate(o)

        @pl.when(o == 0)
        def _():
            third(2)
            fourth(1)
            beside(0)

        @pl.when(o == 1)
        def _():
            beside(1)
            fourth(2)

        @pl.when(o == 2)
        def _():
            beside(2, 3)

    loads[0].wait()

    @pl.loop(0, 4)
    def _(q):
        for j in range(4):

            @pl.when(q == j)
            def _():
                landed(j, (9, 10, 11, 12))

        start = 2 + 2 * q - (q // 3) * 6
        start = start + (1 - (q + 2) // 3) * (ours - 2) + (q // 3) * (theirs - 2)
        pl.loop(start, start + 2)(weigh)
        pl.loop(start, start + 2)(score)

    raw = jnp.concatenate([sc[...], jnp.zeros((128, 96), F32)], axis=1).T[:32]
    pair = iota((32, 128), 0) // REFS
    lane = iota((32, 128), 1) // ROWS
    raw = jnp.where(pair == lane, raw, 0.0)
    scores = raw[:, 0:32] + raw[:, 32:64] + raw[:, 64:96] + raw[:, 96:128]
    scores = scores * (sharp_ref[...].astype(F32) * (1 / math.sqrt(EDGE * PLANE)))
    top = jnp.max(scores, axis=0, keepdims=True)
    expo = jnp.exp(scores - top)
    weights = expo / jnp.sum(expo, axis=0, keepdims=True)
    post_ref[...] = weights[0:8] + weights[8:16] + weights[16:24] + weights[24:32]
    tiled = jnp.concatenate([weights] * 4, axis=1)
    mixed = jnp.where(pair == lane, tiled, 0.0).astype(BF)

    @pl.loop(0, CHUNKS)
    def _(ch):
        got = dot(mixed, y[ch])
        for sub in range(4):
            acc[:, ch * 4 + sub] = got[:, sub * PLANE : (sub + 1) * PLANE].reshape(ORIENTS, REFS, PLANE)

    @pl.loop(0, ORIENTS)
    def _(o):
        cols = pl.ds(pl.multiple_of(o * PLANE, PLANE), PLANE)
        back[:, cols] = dot(bwd[o], acc[o].reshape(256, PLANE).astype(BF)).astype(BF)

    def owner(n, k):
        return (k * SIDE + (n + k) % SIDE) * 2 + core

    def pair_copy(n):
        return remote(out_s.at[n, 1 - core], near.at[n], qs.at[n], qr.at[n], sibling)

    def part_copy(n, k):
        chip = tile // 2
        return remote(both.at[n, k], in_s.at[chip], ps.at[n, k], pr.at[chip], (owner(n, k), z))

    def part_arrival(d):
        chip = (tile // 2 + d) % (TILES // 2)
        return remote(in_s.at[chip], in_s.at[chip], ps.at[0, 0], pr.at[chip], (tile, z))

    def send_parts(n):
        pair_copy(n).wait_recv()
        both[n] = (out_s[n, core].astype(F32) + near[n].astype(F32)).astype(BF)

        @pl.loop(0, SIDE)
        def _(k):
            @pl.when(owner(n, k) != tile)
            def _():
                part_copy(n, k).start()

    @pl.loop(0, 4)
    def _(n):
        cols = pl.ds(pl.multiple_of(n * 256, 256), 256)
        got = dot(back[...], kron[:, :, cols].reshape(ORIENTS * PLANE, 256)).astype(BF)
        for k in range(8):
            out_s[n, k % 2, k // 2] = got[k * 32 : k * 32 + 32]
        pair_copy(n).start()

        @pl.when(n > 0)
        def _():
            send_parts(n - 1)

    send_parts(3)

    @pl.loop(1, TILES // 2)
    def _(d):
        part_arrival(d).wait_recv()

    def add(d, so_far):
        return so_far + in_s[(tile // 2 + d) % (TILES // 2)].astype(F32)

    mine = lax.fori_loop(1, TILES // 2, add, both[(xx - yy + SIDE) % SIDE, yy].astype(F32))
    for block in range(8):
        rows, cols = (block // 2) * 8, (block % 2) * 128
        out_z[:, block, :] = mine[rows : rows + 8, cols : cols + 128]

    def z_copy(d):
        dev = above(d)
        return remote(out_z.at[dev[1]], in_z.at[d], zs.at[d], zr.at[d], dev)

    @pl.loop(1, DEPTH)
    def _(d):
        z_copy(d).start()

    @pl.loop(1, DEPTH)
    def _(d):
        z_copy(d).wait_recv()

    full[tile] = lax.fori_loop(1, DEPTH, lambda d, s: s + in_z[d], out_z[z])

    def full_copy(d):
        return remote(full.at[tile], full.at[tile], fs.at[d], fr.at[d], peer(d))

    @pl.loop(1, TILES)
    def _(d):
        full_copy(d).start()

    @pl.loop(1, DEPTH)
    def _(d):
        z_copy(d).wait_send()

    ref_swap().wait_send()

    @pl.loop(1, DEPTH)
    def _(d):
        ref_copy(d).wait_send()

    for j in range(4):
        for kind in (range(17), range(13), range(13), range(9, 13))[j]:
            step(j, True, kind).wait_send()
            step(j, False, kind).wait_send()

    @pl.loop(0, 4)
    def _(n):
        pair_copy(n).wait_send()

        @pl.loop(0, SIDE)
        def _(k):
            @pl.when(owner(n, k) != tile)
            def _():
                part_copy(n, k).wait_send()

    @pl.loop(1, TILES)
    def _(d):
        full_copy(d).wait_recv()

    whole = full[...].reshape(256, 128)
    mean = jnp.sum(whole * whole) / (EDGE * PLANE)
    scale = 1 / jnp.sqrt(mean + 1e-06)
    for n in range(4):
        for k in range(8):
            got = full[(k // 2 * SIDE + (n + k // 2) % SIDE) * 2 + k % 2]
            for i in range(4):
                spot = (k * 4 + i) * 8 + n * 2
                flat[spot : spot + 2, :] = got[i * 2 : i * 2 + 2]
    upd_ref[...] = (flat[...] * scale).astype(BF)

    @pl.loop(1, TILES)
    def _(d):
        full_copy(d).wait_send()


def shards(subvols, tomogram, sharpness, references, interp, weighting):
    rows, voxels = subvols.shape
    vmem = pl.BlockSpec(memory_space=pltpu.VMEM)
    dma = pltpu.SemaphoreType.DMA
    updated, posterior = pl.pallas_call(
        kernel,
        out_shape=(
            jax.ShapeDtypeStruct((256, 128), BF),
            jax.ShapeDtypeStruct((REFS, rows), F32),
        ),
        in_specs=[pl.BlockSpec(memory_space=pl.ANY)] * 6,
        out_specs=(vmem, vmem),
        scratch_shapes=[
            pltpu.VMEM((rows, voxels), BF),
            pltpu.VMEM((1, rows), jnp.int32),
            pltpu.VMEM((1, rows), BF),
            pltpu.VMEM((1, voxels), BF),
            pltpu.VMEM((ORIENTS, 3, EDGE, EDGE), BF),
            pltpu.VMEM((1, ORIENTS, voxels), BF),
            pltpu.VMEM((CHUNKS, SIDE, SIDE, 2, 16, PLANE), BF),
            pltpu.VMEM((ORIENTS, PLANE, PLANE), BF),
            pltpu.VMEM((REFS, EDGE, PLANE), BF),
            pltpu.VMEM((CHUNKS, 16, PLANE), F32),
            pltpu.VMEM((CHUNKS, ORIENTS * REFS, 4 * PLANE), F32),
            pltpu.VMEM((CHUNKS, ORIENTS * rows, 4 * PLANE), BF),
            pltpu.VMEM((256, 256), BF),
            pltpu.VMEM((EDGE, PLANE), F32),
            pltpu.VMEM((ORIENTS, 256, 256), BF),
            pltpu.VMEM((ORIENTS, 256, 256), BF),
            pltpu.VMEM((128, 32), F32),
            pltpu.VMEM((ORIENTS, EDGE, REFS, PLANE), F32),
            pltpu.VMEM((256, ORIENTS * PLANE), BF),
            pltpu.VMEM((4, 2, SIDE, 32, 256), BF),
            pltpu.VMEM((4, SIDE, 32, 256), BF),
            pltpu.VMEM((4, SIDE, 32, 256), BF),
            pltpu.VMEM((TILES // 2, 32, 256), BF),
            pltpu.VMEM((REFS, 8, 128), F32),
            pltpu.VMEM((DEPTH, 8, 128), F32),
            pltpu.VMEM((TILES, 8, 128), F32),
            pltpu.VMEM((256, 128), F32),
            dma((6,)),
            dma((CHUNKS, 17)),
            dma((CHUNKS, 17)),
            dma((DEPTH,)),
            dma((DEPTH,)),
            dma((4,)),
            dma((4,)),
            dma((4, SIDE)),
            dma((TILES // 2,)),
            dma((DEPTH,)),
            dma((DEPTH,)),
            dma((TILES,)),
            dma((TILES,)),
        ],
        compiler_params=pltpu.CompilerParams(
            collective_id=0, has_side_effects=True, vmem_limit_bytes=56 * 1024 * 1024
        ),
    )(subvols, tomogram.reshape(1, rows), sharpness.reshape(1, rows), references, interp, weighting)
    return updated.reshape(1, voxels), posterior.T


def solution(mesh):
    in_specs = (
        P(("tile", "cls"), None),
        P(("tile", "cls"), None),
        P(("tile", "cls")),
        P("cls", None),
        P(),
        P("tile", None, None),
    )
    out_specs = (P("cls", None), P(("tile", "cls"), None))
    return jax.shard_map(shards, mesh=mesh, in_specs=in_specs, out_specs=out_specs, check_vma=False)
```

```python
import functools
import math

import jax
import jax.numpy as jnp
from jax import lax
from jax.experimental import pallas as pl
from jax.experimental.pallas import tpu as pltpu
from jax.sharding import PartitionSpec as P

F32 = jnp.float32
BF = jnp.bfloat16
MESH = pl.DeviceIdType.MESH
EDGE = 32
PLANE = EDGE * EDGE
SIDE = 4
TILES = 32
DEPTH = 8
ORIENTS = 4
REFS = 8
ROWS = 32
CHUNKS = 8
PAIRS = 3
NT = (((1,), (1,)), ((), ()))


def dot(a, b):
    return jnp.dot(a, b, preferred_element_type=F32)


def dot_nt(a, b):
    return lax.dot_general(a, b, NT, preferred_element_type=F32)


def iota(shape, dim):
    return lax.broadcasted_iota(jnp.int32, shape, dim)


def mask(cond):
    return jnp.where(cond, 1.0, 0.0).astype(BF)


def kernel(
    x_hbm, tom_hbm, sharp_hbm, own_hbm, interp_hbm, w_hbm,
    upd_ref, post_ref,
    x_ref, tom_ref, sharp_ref, own_ref, interp_ref, w_ref,
    wall, kron, cur, stage, rot, y, pick, rep, fwd, bwd, sc, acc, back,
    out_s, near, both, in_s, out_z, in_z, full, flat,
    ls, ws, wr, rs, rr, qs, qr, ps, pr, zs, zr, fs, fr,
):
    places = (x_ref, tom_ref, sharp_ref, own_ref, interp_ref, w_ref)
    loads = [
        pltpu.make_async_copy(source, place, ls.at[n])
        for n, (source, place) in enumerate(zip((x_hbm, tom_hbm, sharp_hbm, own_hbm, interp_hbm, w_hbm), places))
    ]
    for n in (5, 3, 4, 1, 2, 0):
        loads[n].start()

    tile, z = lax.axis_index("tile"), lax.axis_index("cls")
    core, xx, yy = tile % 2, (tile // 2) % SIDE, tile // (2 * SIDE)

    def at(y_, x_, c_):
        return ((y_ * SIDE + x_) * 2 + c_, z)

    sibling = (tile + 1 - 2 * core, z)

    def peer(d):
        return ((tile + d) % TILES, z)

    def above(d):
        return (tile, (z + d) % DEPTH)

    def remote(src, dst, ssem, rsem, dev):
        return pltpu.make_async_remote_copy(
            src_ref=src, dst_ref=dst, send_sem=ssem, recv_sem=rsem, device_id=dev, device_id_type=MESH
        )

    barrier = pltpu.get_barrier_semaphore()

    @pl.loop(1, TILES)
    def _(d):
        pl.semaphore_signal(barrier, inc=1, device_id=peer(d), device_id_type=MESH)

    @pl.loop(1, DEPTH)
    def _(d):
        pl.semaphore_signal(barrier, inc=1, device_id=above(d), device_id_type=MESH)

    loads[3].wait()
    loads[5].wait()
    for a in range(EDGE):
        cols = slice(a * PLANE, (a + 1) * PLANE)
        stage[a // 4, (a % 4) * 4 : (a % 4) * 4 + 4, :] = w_ref[0, :, cols].astype(F32)
        rep[a : a + 1, :] = own_ref[:, cols].astype(F32)
    mine_first = pl.ds(2 - 2 * (z % 2), 2)
    wall[mine_first, 0, 0, core] = stage[mine_first].astype(BF)
    wall[4:, 0, 0, core] = stage[4:].astype(BF)
    half = pl.ds(pl.multiple_of(core * 16, 16), 16)
    cur[z, half] = rep[half, :].astype(BF)

    pl.semaphore_wait(barrier, TILES - 1 + DEPTH - 1)

    def ref_copy(d):
        return remote(cur.at[z, half], cur.at[z, half], rs.at[d], rr.at[d], above(d))

    def ref_swap():
        return remote(cur.at[:, half], cur.at[:, half], rs.at[0], rr.at[0], sibling)

    ours, theirs = 2 - 2 * (z % 2), 2 * (z % 2)
    HOPS, LANDS = (1, -1, 2), (3, 1, 2)

    def chunk(j, xfirst):
        start = (ours, 4, 6, theirs)[j]
        return start if xfirst else start + 1

    def step(j, xfirst, kind):
        ch = chunk(j, xfirst)

        def block(line, place):
            return wall.at[ch, line, place, core] if xfirst else wall.at[ch, place, line, core]

        def along(first, hop):
            if first == xfirst:
                return at(yy, (xx + hop + SIDE) % SIDE, core)
            return at((yy + hop + SIDE) % SIDE, xx, core)

        rest = pl.ds(1, 3)
        if kind < 3:
            source, target, dev = block(0, 0), block(0, LANDS[kind]), along(True, HOPS[kind])
        elif kind < 6:
            source, target, dev = block(0, 0), block(LANDS[kind - 3], 0), along(False, HOPS[kind - 3])
        elif kind == 8 and j < PAIRS - 1:
            sign = 1 - 2 * (j % 2)
            source, target, dev = block(2 + sign, rest), block(2, rest), along(False, sign)
        elif kind < 9:
            source, target, dev = block(0, rest), block(LANDS[kind - 6], rest), along(False, HOPS[kind - 6])
        else:
            source = target = block((0, 3, 1, 2)[(kind - 9) % 4], pl.ds(0, 4))
            dev = sibling if kind < 13 else above(1 if xfirst else DEPTH - 1)
        return remote(source, target, ws.at[ch, kind], wr.at[ch, kind], dev)

    def go(j, kinds):
        for kind in kinds:
            step(j, True, kind).start()
            step(j, False, kind).start()

    def landed(j, kinds):
        for kind in kinds:
            step(j, True, kind).wait_recv()
            step(j, False, kind).wait_recv()

    def second(j):
        landed(j, (0, 1, 2))
        go(j, ((13, 6, 7, 9), (6, 7, 9), (6, 7, 8, 9))[j])

    def third(j):
        landed(j, (3, 4, 6, 7))
        go(j, ((8, 14, 15, 10, 11), (8, 10, 11), (10, 11))[j])

    def fourth(j):
        landed(j, (5, 8))
        go(j, ((16, 12), (12,), (12,))[j])

    def beside(*lines):
        for line in lines:
            landed(3, (13 + line,))
            go(3, (9 + line,))

    def build(o):
        a1 = dot(interp_ref[o, 1], mask(iota((EDGE, PLANE), 1) // EDGE == iota((EDGE, PLANE), 0)))
        a2 = dot(interp_ref[o, 2], mask(iota((EDGE, PLANE), 1) % EDGE == iota((EDGE, PLANE), 0)))
        rep[...] = a1

        @pl.loop(0, EDGE)
        def _(b):
            kron[o, pl.ds(pl.multiple_of(b * EDGE, EDGE), EDGE), :] = (rep[pl.ds(b, 1), :] * a2).astype(BF)

        a0 = interp_ref[o, 0]
        select = mask(iota((256, EDGE), 0) // REFS == iota((256, EDGE), 1))
        row, col = iota((256, 256), 0), iota((256, 256), 1)
        spread = mask(iota((EDGE, 256), 1) % EDGE == iota((EDGE, 256), 0))
        wide = dot(dot(select, a0).astype(BF), spread)
        fwd[o] = jnp.where(row % REFS == col // EDGE, wide, 0.0).astype(BF)
        spread = mask(iota((EDGE, 256), 1) // REFS == iota((EDGE, 256), 0))
        wide = dot(dot_nt(select, a0).astype(BF), spread)
        bwd[o] = jnp.where(row % REFS == col % REFS, wide, 0.0).astype(BF)

    def rotate(o):
        volumes = cur[...].reshape(256, PLANE)
        for n in range(4):
            cols = slice(n * 256, (n + 1) * 256)
            part = dot_nt(volumes, kron[o, cols, :]).astype(BF)
            got = dot(fwd[o], part).reshape(CHUNKS, 4, REFS, 256)
            for sub in range(4):
                spot = slice(sub * PLANE + n * 256, sub * PLANE + (n + 1) * 256)
                rot[:, pl.ds(pl.multiple_of(o * REFS, REFS), REFS), spot] = got[:, sub]

    def weigh(ch):
        for h in range(2):
            for n in range(4):
                cols = slice(n * 256, (n + 1) * 256)
                got = dot(pick[...], wall[ch, :, :, :, h * 8 : h * 8 + 8, cols].reshape(256, 256))
                for sub in range(2):
                    spot = (h * 2 + sub) * PLANE + n * 256
                    rows = x_ref[:, pl.ds(pl.multiple_of(ch * 4 * PLANE + spot, 256), 256)].astype(F32)
                    prod = got[sub * 128 : sub * 128 + 128].reshape(ORIENTS, ROWS, 256) * rows[None]
                    y[ch, :, spot : spot + 256] = prod.reshape(128, 256).astype(BF)

    def score(ch):
        sc[...] += dot_nt(y[ch], rot[ch].astype(BF))

    go(0, (0, 1, 2, 3, 4, 5))
    go(1, (0, 1, 2))

    @pl.loop(1, DEPTH)
    def _(d):
        ref_copy(d).start()

    loads[4].wait()

    @pl.loop(0, ORIENTS)
    def _(o):
        build(o)

        @pl.when(o == 1)
        def _():
            second(0)
            go(1, (3, 4, 5))
            go(2, (0, 1, 2))

    second(1)
    loads[1].wait()
    loads[2].wait()
    sc[...] = jnp.zeros_like(sc)
    diagonal = iota((ROWS, ROWS), 0) == iota((ROWS, ROWS), 1)
    named = jnp.sum(jnp.where(diagonal, tom_ref[...].astype(F32), 0.0), axis=1, keepdims=True).astype(jnp.int32)
    away_y = (named // (2 * SIDE) + SIDE - yy) % SIDE
    away_x = (named // 2 + SIDE - xx) % SIDE
    named = (away_y * SIDE + away_x) * 2 + named % 2
    for sub in range(2):
        for o in range(ORIENTS):
            code = named * 8 + (sub * 4 + o)
            pick[pl.ds((sub * 4 + o) * ROWS, ROWS), :] = mask(code == iota((ROWS, 256), 1))
    third(0)
    go(2, (3, 4, 5))
    second(2)

    @pl.loop(1, DEPTH)
    def _(d):
        ref_copy(d).wait_recv()

    ref_swap().start()
    ref_swap().wait_recv()

    @pl.loop(0, ORIENTS)
    def _(o):
        rotate(o)

        @pl.when(o == 0)
        def _():
            fourth(0)

        @pl.when(o == 1)
        def _():
            third(1)
            beside(0)

        @pl.when(o == 2)
        def _():
            third(2)
            beside(1)

        @pl.when(o == 3)
        def _():
            fourth(1)
            beside(2)

    loads[0].wait()

    @pl.loop(0, 4)
    def _(q):
        @pl.when(q == 0)
        def _():
            landed(0, (9, 10, 11, 12))

        @pl.when(q == 1)
        def _():
            landed(1, (9, 10, 11, 12))
            beside(3)

        @pl.when(q == 2)
        def _():
            fourth(2)
            landed(3, (9, 10, 11, 12))

        @pl.when(q == 3)
        def _():
            landed(2, (9, 10, 11, 12))

        start = (q % 2) * (3 + q) + (1 - q % 2) * (ours + (q // 2) * (theirs - ours))
        pl.loop(start, start + 2)(weigh)
        pl.loop(start, start + 2)(score)

    raw = jnp.concatenate([sc[...], jnp.zeros((128, 96), F32)], axis=1).T[:32]
    pair = iota((32, 128), 0) // REFS
    lane = iota((32, 128), 1) // ROWS
    raw = jnp.where(pair == lane, raw, 0.0)
    scores = raw[:, 0:32] + raw[:, 32:64] + raw[:, 64:96] + raw[:, 96:128]
    scores = scores * (sharp_ref[...].astype(F32) * (1 / math.sqrt(EDGE * PLANE)))
    top = jnp.max(scores, axis=0, keepdims=True)
    expo = jnp.exp(scores - top)
    weights = expo / jnp.sum(expo, axis=0, keepdims=True)
    post_ref[...] = weights[0:8] + weights[8:16] + weights[16:24] + weights[24:32]
    tiled = jnp.concatenate([weights] * 4, axis=1)
    mixed = jnp.where(pair == lane, tiled, 0.0).astype(BF)

    @pl.loop(0, CHUNKS)
    def _(ch):
        got = dot(mixed, y[ch])
        for sub in range(4):
            acc[:, ch * 4 + sub] = got[:, sub * PLANE : (sub + 1) * PLANE].reshape(ORIENTS, REFS, PLANE)

    @pl.loop(0, ORIENTS)
    def _(o):
        cols = pl.ds(pl.multiple_of(o * PLANE, PLANE), PLANE)
        back[:, cols] = dot(bwd[o], acc[o].reshape(256, PLANE).astype(BF)).astype(BF)

    def owner(n, k):
        return (k * SIDE + (n + k) % SIDE) * 2 + core

    def pair_copy(n):
        return remote(out_s.at[n, 1 - core], near.at[n], qs.at[n], qr.at[n], sibling)

    def part_copy(n, k):
        chip = tile // 2
        return remote(both.at[n, k], in_s.at[chip], ps.at[n, k], pr.at[chip], (owner(n, k), z))

    def part_arrival(d):
        chip = (tile // 2 + d) % (TILES // 2)
        return remote(in_s.at[chip], in_s.at[chip], ps.at[0, 0], pr.at[chip], (tile, z))

    def send_parts(n):
        pair_copy(n).wait_recv()
        both[n] = (out_s[n, core].astype(F32) + near[n].astype(F32)).astype(BF)

        @pl.loop(0, SIDE)
        def _(k):
            @pl.when(owner(n, k) != tile)
            def _():
                part_copy(n, k).start()

    @pl.loop(0, 4)
    def _(n):
        cols = pl.ds(pl.multiple_of(n * 256, 256), 256)
        got = dot(back[...], kron[:, :, cols].reshape(ORIENTS * PLANE, 256)).astype(BF)
        for k in range(8):
            out_s[n, k % 2, k // 2] = got[k * 32 : k * 32 + 32]
        pair_copy(n).start()

        @pl.when(n > 0)
        def _():
            send_parts(n - 1)

    send_parts(3)

    def add(d, so_far):
        part_arrival(d).wait_recv()
        return so_far + in_s[(tile // 2 + d) % (TILES // 2)].astype(F32)

    mine = lax.fori_loop(1, TILES // 2, add, both[(xx - yy + SIDE) % SIDE, yy].astype(F32))
    for block in range(8):
        rows, cols = (block // 2) * 8, (block % 2) * 128
        out_z[:, block, :] = mine[rows : rows + 8, cols : cols + 128]

    def z_copy(d):
        dev = above(d)
        return remote(out_z.at[dev[1]], in_z.at[d], zs.at[d], zr.at[d], dev)

    @pl.loop(1, DEPTH)
    def _(d):
        z_copy(d).start()

    @pl.loop(1, DEPTH)
    def _(d):
        z_copy(d).wait_recv()

    full[tile] = lax.fori_loop(1, DEPTH, lambda d, s: s + in_z[d], out_z[z])

    def full_copy(d):
        return remote(full.at[tile], full.at[tile], fs.at[d], fr.at[d], peer(d))

    @pl.loop(1, TILES)
    def _(d):
        full_copy(d).start()

    @pl.loop(1, DEPTH)
    def _(d):
        z_copy(d).wait_send()

    ref_swap().wait_send()

    @pl.loop(1, DEPTH)
    def _(d):
        ref_copy(d).wait_send()

    for j in range(4):
        for kind in (range(17), range(13), range(13), range(9, 13))[j]:
            step(j, True, kind).wait_send()
            step(j, False, kind).wait_send()

    @pl.loop(0, 4)
    def _(n):
        pair_copy(n).wait_send()

        @pl.loop(0, SIDE)
        def _(k):
            @pl.when(owner(n, k) != tile)
            def _():
                part_copy(n, k).wait_send()

    @pl.loop(1, TILES)
    def _(d):
        full_copy(d).wait_recv()

    whole = full[...].reshape(256, 128)
    mean = jnp.sum(whole * whole) / (EDGE * PLANE)
    scale = 1 / jnp.sqrt(mean + 1e-06)
    for n in range(4):
        for k in range(8):
            got = full[(k // 2 * SIDE + (n + k // 2) % SIDE) * 2 + k % 2]
            for i in range(4):
                spot = (k * 4 + i) * 8 + n * 2
                flat[spot : spot + 2, :] = got[i * 2 : i * 2 + 2]
    upd_ref[...] = (flat[...] * scale).astype(BF)

    @pl.loop(1, TILES)
    def _(d):
        full_copy(d).wait_send()


def shards(subvols, tomogram, sharpness, references, interp, weighting):
    rows, voxels = subvols.shape
    vmem = pl.BlockSpec(memory_space=pltpu.VMEM)
    dma = pltpu.SemaphoreType.DMA
    updated, posterior = pl.pallas_call(
        kernel,
        out_shape=(
            jax.ShapeDtypeStruct((256, 128), BF),
            jax.ShapeDtypeStruct((REFS, rows), F32),
        ),
        in_specs=[pl.BlockSpec(memory_space=pl.ANY)] * 6,
        out_specs=(vmem, vmem),
        scratch_shapes=[
            pltpu.VMEM((rows, voxels), BF),
            pltpu.VMEM((1, rows), jnp.int32),
            pltpu.VMEM((1, rows), BF),
            pltpu.VMEM((1, voxels), BF),
            pltpu.VMEM((ORIENTS, 3, EDGE, EDGE), BF),
            pltpu.VMEM((1, ORIENTS, voxels), BF),
            pltpu.VMEM((CHUNKS, SIDE, SIDE, 2, 16, PLANE), BF),
            pltpu.VMEM((ORIENTS, PLANE, PLANE), BF),
            pltpu.VMEM((REFS, EDGE, PLANE), BF),
            pltpu.VMEM((CHUNKS, 16, PLANE), F32),
            pltpu.VMEM((CHUNKS, ORIENTS * REFS, 4 * PLANE), F32),
            pltpu.VMEM((CHUNKS, ORIENTS * rows, 4 * PLANE), BF),
            pltpu.VMEM((256, 256), BF),
            pltpu.VMEM((EDGE, PLANE), F32),
            pltpu.VMEM((ORIENTS, 256, 256), BF),
            pltpu.VMEM((ORIENTS, 256, 256), BF),
            pltpu.VMEM((128, 32), F32),
            pltpu.VMEM((ORIENTS, EDGE, REFS, PLANE), F32),
            pltpu.VMEM((256, ORIENTS * PLANE), BF),
            pltpu.VMEM((4, 2, SIDE, 32, 256), BF),
            pltpu.VMEM((4, SIDE, 32, 256), BF),
            pltpu.VMEM((4, SIDE, 32, 256), BF),
            pltpu.VMEM((TILES // 2, 32, 256), BF),
            pltpu.VMEM((REFS, 8, 128), F32),
            pltpu.VMEM((DEPTH, 8, 128), F32),
            pltpu.VMEM((TILES, 8, 128), F32),
            pltpu.VMEM((256, 128), F32),
            dma((6,)),
            dma((CHUNKS, 17)),
            dma((CHUNKS, 17)),
            dma((DEPTH,)),
            dma((DEPTH,)),
            dma((4,)),
            dma((4,)),
            dma((4, SIDE)),
            dma((TILES // 2,)),
            dma((DEPTH,)),
            dma((DEPTH,)),
            dma((TILES,)),
            dma((TILES,)),
        ],
        compiler_params=pltpu.CompilerParams(
            collective_id=0, has_side_effects=True, vmem_limit_bytes=56 * 1024 * 1024
        ),
    )(subvols, tomogram.reshape(1, rows), sharpness.reshape(1, rows), references, interp, weighting)
    return updated.reshape(1, voxels), posterior.T


def solution(mesh):
    in_specs = (
        P(("tile", "cls"), None),
        P(("tile", "cls"), None),
        P(("tile", "cls")),
        P("cls", None),
        P(),
        P("tile", None, None),
    )
    out_specs = (P("cls", None), P(("tile", "cls"), None))
    return jax.shard_map(shards, mesh=mesh, in_specs=in_specs, out_specs=out_specs, check_vma=False)
```

```python
import functools
import math

import jax
import jax.numpy as jnp
from jax import lax
from jax.experimental import pallas as pl
from jax.experimental.pallas import tpu as pltpu
from jax.sharding import PartitionSpec as P

F32 = jnp.float32
BF = jnp.bfloat16
MESH = pl.DeviceIdType.MESH
EDGE = 32
PLANE = EDGE * EDGE
SIDE = 4
TILES = 32
DEPTH = 8
ORIENTS = 4
REFS = 8
ROWS = 32
CHUNKS = 8
PAIRS = 3
NT = (((1,), (1,)), ((), ()))


def dot(a, b):
    return jnp.dot(a, b, preferred_element_type=F32)


def dot_nt(a, b):
    return lax.dot_general(a, b, NT, preferred_element_type=F32)


def iota(shape, dim):
    return lax.broadcasted_iota(jnp.int32, shape, dim)


def mask(cond):
    return jnp.where(cond, 1.0, 0.0).astype(BF)


def kernel(
    x_hbm, tom_hbm, sharp_hbm, own_hbm, interp_hbm, w_hbm,
    upd_ref, post_ref,
    x_ref, tom_ref, sharp_ref, own_ref, interp_ref, w_ref,
    wall, kron, cur, stage, rot, y, pick, rep, fwd, bwd, sc, acc, back,
    out_s, near, both, in_s, out_z, in_z, full, flat,
    ls, ws, wr, rs, rr, qs, qr, ps, pr, zs, zr, fs, fr,
):
    places = (x_ref, tom_ref, sharp_ref, own_ref, interp_ref, w_ref)
    loads = [
        pltpu.make_async_copy(source, place, ls.at[n])
        for n, (source, place) in enumerate(zip((x_hbm, tom_hbm, sharp_hbm, own_hbm, interp_hbm, w_hbm), places))
    ]
    for n in (5, 3, 4, 1, 2, 0):
        loads[n].start()

    tile, z = lax.axis_index("tile"), lax.axis_index("cls")
    core, xx, yy = tile % 2, (tile // 2) % SIDE, tile // (2 * SIDE)

    def at(y_, x_, c_):
        return ((y_ * SIDE + x_) * 2 + c_, z)

    sibling = (tile + 1 - 2 * core, z)

    def peer(d):
        return ((tile + d) % TILES, z)

    def above(d):
        return (tile, (z + d) % DEPTH)

    def remote(src, dst, ssem, rsem, dev):
        return pltpu.make_async_remote_copy(
            src_ref=src, dst_ref=dst, send_sem=ssem, recv_sem=rsem, device_id=dev, device_id_type=MESH
        )

    barrier = pltpu.get_barrier_semaphore()

    @pl.loop(1, TILES)
    def _(d):
        pl.semaphore_signal(barrier, inc=1, device_id=peer(d), device_id_type=MESH)

    @pl.loop(1, DEPTH)
    def _(d):
        pl.semaphore_signal(barrier, inc=1, device_id=above(d), device_id_type=MESH)

    loads[3].wait()
    loads[5].wait()
    for a in range(EDGE):
        cols = slice(a * PLANE, (a + 1) * PLANE)
        stage[a // 4, (a % 4) * 4 : (a % 4) * 4 + 4, :] = w_ref[0, :, cols].astype(F32)
        rep[a : a + 1, :] = own_ref[:, cols].astype(F32)
    mine_first = pl.ds(2 - 2 * (z % 2), 2)
    wall[mine_first, 0, 0, core] = stage[mine_first].astype(BF)
    wall[4:, 0, 0, core] = stage[4:].astype(BF)
    half = pl.ds(pl.multiple_of(core * 16, 16), 16)
    cur[z, half] = rep[half, :].astype(BF)

    pl.semaphore_wait(barrier, TILES - 1 + DEPTH - 1)

    def ref_copy(d):
        return remote(cur.at[z, half], cur.at[z, half], rs.at[d], rr.at[d], above(d))

    def ref_swap():
        return remote(cur.at[:, half], cur.at[:, half], rs.at[0], rr.at[0], sibling)

    ours, theirs = 2 - 2 * (z % 2), 2 * (z % 2)
    HOPS, LANDS = (1, -1, 2), (3, 1, 2)

    def chunk(j, xfirst):
        start = (ours, 4, 6, theirs)[j]
        return start if xfirst else start + 1

    def step(j, xfirst, kind):
        ch = chunk(j, xfirst)

        def block(line, place):
            return wall.at[ch, line, place, core] if xfirst else wall.at[ch, place, line, core]

        def along(first, hop):
            if first == xfirst:
                return at(yy, (xx + hop + SIDE) % SIDE, core)
            return at((yy + hop + SIDE) % SIDE, xx, core)

        rest = pl.ds(1, 3)
        if kind < 3:
            source, target, dev = block(0, 0), block(0, LANDS[kind]), along(True, HOPS[kind])
        elif kind < 6:
            source, target, dev = block(0, 0), block(LANDS[kind - 3], 0), along(False, HOPS[kind - 3])
        elif kind == 8 and j < PAIRS - 1:
            sign = 1 - 2 * (j % 2)
            source, target, dev = block(2 + sign, rest), block(2, rest), along(False, sign)
        elif kind < 9:
            source, target, dev = block(0, rest), block(LANDS[kind - 6], rest), along(False, HOPS[kind - 6])
        else:
            source = target = block((0, 3, 1, 2)[(kind - 9) % 4], pl.ds(0, 4))
            dev = sibling if kind < 13 else above(1 if xfirst else DEPTH - 1)
        return remote(source, target, ws.at[ch, kind], wr.at[ch, kind], dev)

    def go(j, kinds):
        for kind in kinds:
            step(j, True, kind).start()
            step(j, False, kind).start()

    def landed(j, kinds):
        for kind in kinds:
            step(j, True, kind).wait_recv()
            step(j, False, kind).wait_recv()

    def second(j):
        landed(j, (0, 1, 2))
        go(j, ((13, 6, 7, 9), (6, 7, 9), (6, 7, 8, 9))[j])

    def third(j):
        landed(j, (3, 4, 6, 7))
        go(j, ((8, 14, 15, 10, 11), (8, 10, 11), (10, 11))[j])

    def fourth(j):
        landed(j, (5, 8))
        go(j, ((16, 12), (12,), (12,))[j])

    def beside(*lines):
        for line in lines:
            landed(3, (13 + line,))
            go(3, (9 + line,))

    def build(o):
        a1 = dot(interp_ref[o, 1], mask(iota((EDGE, PLANE), 1) // EDGE == iota((EDGE, PLANE), 0)))
        a2 = dot(interp_ref[o, 2], mask(iota((EDGE, PLANE), 1) % EDGE == iota((EDGE, PLANE), 0)))
        rep[...] = a1

        @pl.loop(0, EDGE)
        def _(b):
            kron[o, pl.ds(pl.multiple_of(b * EDGE, EDGE), EDGE), :] = (rep[pl.ds(b, 1), :] * a2).astype(BF)

        a0 = interp_ref[o, 0]
        select = mask(iota((256, EDGE), 0) // REFS == iota((256, EDGE), 1))
        row, col = iota((256, 256), 0), iota((256, 256), 1)
        spread = mask(iota((EDGE, 256), 1) % EDGE == iota((EDGE, 256), 0))
        wide = dot(dot(select, a0).astype(BF), spread)
        fwd[o] = jnp.where(row % REFS == col // EDGE, wide, 0.0).astype(BF)
        spread = mask(iota((EDGE, 256), 1) // REFS == iota((EDGE, 256), 0))
        wide = dot(dot_nt(select, a0).astype(BF), spread)
        bwd[o] = jnp.where(row % REFS == col % REFS, wide, 0.0).astype(BF)

    def rotate(o):
        volumes = cur[...].reshape(256, PLANE)
        for n in range(4):
            cols = slice(n * 256, (n + 1) * 256)
            part = dot_nt(volumes, kron[o, cols, :]).astype(BF)
            got = dot(fwd[o], part).reshape(CHUNKS, 4, REFS, 256)
            for sub in range(4):
                spot = slice(sub * PLANE + n * 256, sub * PLANE + (n + 1) * 256)
                rot[:, pl.ds(pl.multiple_of(o * REFS, REFS), REFS), spot] = got[:, sub]

    def weigh(ch):
        for h in range(2):
            for n in range(4):
                cols = slice(n * 256, (n + 1) * 256)
                got = dot(pick[...], wall[ch, :, :, :, h * 8 : h * 8 + 8, cols].reshape(256, 256))
                for sub in range(2):
                    spot = (h * 2 + sub) * PLANE + n * 256
                    rows = x_ref[:, pl.ds(pl.multiple_of(ch * 4 * PLANE + spot, 256), 256)].astype(F32)
                    prod = got[sub * 128 : sub * 128 + 128].reshape(ORIENTS, ROWS, 256) * rows[None]
                    y[ch, :, spot : spot + 256] = prod.reshape(128, 256).astype(BF)

    def score(ch):
        sc[...] += dot_nt(y[ch], rot[ch].astype(BF))

    go(0, (0, 1, 2, 3, 4, 5))
    go(1, (0, 1, 2))

    @pl.loop(1, DEPTH)
    def _(d):
        ref_copy(d).start()

    loads[4].wait()

    @pl.loop(0, ORIENTS)
    def _(o):
        build(o)

        @pl.when(o == 1)
        def _():
            second(0)
            go(1, (3, 4, 5))
            go(2, (0, 1, 2))

    second(1)
    loads[1].wait()
    loads[2].wait()
    sc[...] = jnp.zeros_like(sc)
    diagonal = iota((ROWS, ROWS), 0) == iota((ROWS, ROWS), 1)
    named = jnp.sum(jnp.where(diagonal, tom_ref[...].astype(F32), 0.0), axis=1, keepdims=True).astype(jnp.int32)
    away_y = (named // (2 * SIDE) + SIDE - yy) % SIDE
    away_x = (named // 2 + SIDE - xx) % SIDE
    named = (away_y * SIDE + away_x) * 2 + named % 2
    for sub in range(2):
        for o in range(ORIENTS):
            code = named * 8 + (sub * 4 + o)
            pick[pl.ds((sub * 4 + o) * ROWS, ROWS), :] = mask(code == iota((ROWS, 256), 1))
    third(0)
    go(2, (3, 4, 5))
    second(2)

    @pl.loop(1, DEPTH)
    def _(d):
        ref_copy(d).wait_recv()

    ref_swap().start()
    ref_swap().wait_recv()

    @pl.loop(0, ORIENTS)
    def _(o):
        rotate(o)

        @pl.when(o == 0)
        def _():
            fourth(0)

        @pl.when(o == 1)
        def _():
            third(1)
            beside(0)

        @pl.when(o == 2)
        def _():
            third(2)
            beside(1)

        @pl.when(o == 3)
        def _():
            fourth(1)
            beside(2)

    loads[0].wait()

    @pl.loop(0, 4)
    def _(q):
        @pl.when(q == 0)
        def _():
            landed(0, (9, 10, 11, 12))

        @pl.when(q == 1)
        def _():
            landed(1, (9, 10, 11, 12))
            beside(3)

        @pl.when(q == 2)
        def _():
            fourth(2)
            landed(3, (9, 10, 11, 12))

        @pl.when(q == 3)
        def _():
            landed(2, (9, 10, 11, 12))

        start = (q % 2) * (3 + q) + (1 - q % 2) * (ours + (q // 2) * (theirs - ours))
        pl.loop(start, start + 2)(weigh)
        pl.loop(start, start + 2)(score)

    raw = jnp.concatenate([sc[...], jnp.zeros((128, 96), F32)], axis=1).T[:32]
    pair = iota((32, 128), 0) // REFS
    lane = iota((32, 128), 1) // ROWS
    raw = jnp.where(pair == lane, raw, 0.0)
    scores = raw[:, 0:32] + raw[:, 32:64] + raw[:, 64:96] + raw[:, 96:128]
    scores = scores * (sharp_ref[...].astype(F32) * (1 / math.sqrt(EDGE * PLANE)))
    top = jnp.max(scores, axis=0, keepdims=True)
    expo = jnp.exp(scores - top)
    weights = expo / jnp.sum(expo, axis=0, keepdims=True)
    post_ref[...] = weights[0:8] + weights[8:16] + weights[16:24] + weights[24:32]
    tiled = jnp.concatenate([weights] * 4, axis=1)
    mixed = jnp.where(pair == lane, tiled, 0.0).astype(BF)

    @pl.loop(0, CHUNKS, unroll=4)
    def _(ch):
        got = dot(mixed, y[ch])
        for sub in range(4):
            acc[:, ch * 4 + sub] = got[:, sub * PLANE : (sub + 1) * PLANE].reshape(ORIENTS, REFS, PLANE)

    @pl.loop(0, ORIENTS, unroll=2)
    def _(o):
        cols = pl.ds(pl.multiple_of(o * PLANE, PLANE), PLANE)
        back[:, cols] = dot(bwd[o], acc[o].reshape(256, PLANE).astype(BF)).astype(BF)

    def owner(n, k):
        return (k * SIDE + (n + k) % SIDE) * 2 + core

    def pair_copy(n):
        return remote(out_s.at[n, 1 - core], near.at[n], qs.at[n], qr.at[n], sibling)

    def part_copy(n, k):
        chip = tile // 2
        return remote(both.at[n, k], in_s.at[chip], ps.at[n, k], pr.at[chip], (owner(n, k), z))

    def part_arrival(d):
        chip = (tile // 2 + d) % (TILES // 2)
        return remote(in_s.at[chip], in_s.at[chip], ps.at[0, 0], pr.at[chip], (tile, z))

    def send_parts(n):
        pair_copy(n).wait_recv()
        both[n] = (out_s[n, core].astype(F32) + near[n].astype(F32)).astype(BF)

        @pl.loop(0, SIDE)
        def _(k):
            @pl.when(owner(n, k) != tile)
            def _():
                part_copy(n, k).start()

    @pl.loop(0, 4)
    def _(n):
        cols = pl.ds(pl.multiple_of(n * 256, 256), 256)
        got = dot(back[...], kron[:, :, cols].reshape(ORIENTS * PLANE, 256)).astype(BF)
        for k in range(8):
            out_s[n, k % 2, k // 2] = got[k * 32 : k * 32 + 32]
        pair_copy(n).start()

        @pl.when(n > 0)
        def _():
            send_parts(n - 1)

    send_parts(3)

    def add(d, so_far):
        part_arrival(d).wait_recv()
        return so_far + in_s[(tile // 2 + d) % (TILES // 2)].astype(F32)

    mine = lax.fori_loop(1, TILES // 2, add, both[(xx - yy + SIDE) % SIDE, yy].astype(F32))
    for block in range(8):
        rows, cols = (block // 2) * 8, (block % 2) * 128
        out_z[:, block, :] = mine[rows : rows + 8, cols : cols + 128]

    def z_copy(d):
        dev = above(d)
        return remote(out_z.at[dev[1]], in_z.at[d], zs.at[d], zr.at[d], dev)

    @pl.loop(1, DEPTH)
    def _(d):
        z_copy(d).start()

    @pl.loop(1, DEPTH)
    def _(d):
        z_copy(d).wait_recv()

    full[tile] = lax.fori_loop(1, DEPTH, lambda d, s: s + in_z[d], out_z[z])

    def full_copy(d):
        return remote(full.at[tile], full.at[tile], fs.at[d], fr.at[d], peer(d))

    @pl.loop(1, TILES)
    def _(d):
        full_copy(d).start()

    @pl.loop(1, DEPTH)
    def _(d):
        z_copy(d).wait_send()

    ref_swap().wait_send()

    @pl.loop(1, DEPTH)
    def _(d):
        ref_copy(d).wait_send()

    for j in range(4):
        for kind in (range(17), range(13), range(13), range(9, 13))[j]:
            step(j, True, kind).wait_send()
            step(j, False, kind).wait_send()

    @pl.loop(0, 4)
    def _(n):
        pair_copy(n).wait_send()

        @pl.loop(0, SIDE)
        def _(k):
            @pl.when(owner(n, k) != tile)
            def _():
                part_copy(n, k).wait_send()

    @pl.loop(1, TILES)
    def _(d):
        full_copy(d).wait_recv()

    whole = full[...].reshape(256, 128)
    mean = jnp.sum(whole * whole) / (EDGE * PLANE)
    scale = 1 / jnp.sqrt(mean + 1e-06)
    for n in range(4):
        for k in range(8):
            got = full[(k // 2 * SIDE + (n + k // 2) % SIDE) * 2 + k % 2]
            for i in range(4):
                spot = (k * 4 + i) * 8 + n * 2
                flat[spot : spot + 2, :] = got[i * 2 : i * 2 + 2]
    upd_ref[...] = (flat[...] * scale).astype(BF)

    @pl.loop(1, TILES)
    def _(d):
        full_copy(d).wait_send()


def shards(subvols, tomogram, sharpness, references, interp, weighting):
    rows, voxels = subvols.shape
    vmem = pl.BlockSpec(memory_space=pltpu.VMEM)
    dma = pltpu.SemaphoreType.DMA
    updated, posterior = pl.pallas_call(
        kernel,
        out_shape=(
            jax.ShapeDtypeStruct((256, 128), BF),
            jax.ShapeDtypeStruct((REFS, rows), F32),
        ),
        in_specs=[pl.BlockSpec(memory_space=pl.ANY)] * 6,
        out_specs=(vmem, vmem),
        scratch_shapes=[
            pltpu.VMEM((rows, voxels), BF),
            pltpu.VMEM((1, rows), jnp.int32),
            pltpu.VMEM((1, rows), BF),
            pltpu.VMEM((1, voxels), BF),
            pltpu.VMEM((ORIENTS, 3, EDGE, EDGE), BF),
            pltpu.VMEM((1, ORIENTS, voxels), BF),
            pltpu.VMEM((CHUNKS, SIDE, SIDE, 2, 16, PLANE), BF),
            pltpu.VMEM((ORIENTS, PLANE, PLANE), BF),
            pltpu.VMEM((REFS, EDGE, PLANE), BF),
            pltpu.VMEM((CHUNKS, 16, PLANE), F32),
            pltpu.VMEM((CHUNKS, ORIENTS * REFS, 4 * PLANE), F32),
            pltpu.VMEM((CHUNKS, ORIENTS * rows, 4 * PLANE), BF),
            pltpu.VMEM((256, 256), BF),
            pltpu.VMEM((EDGE, PLANE), F32),
            pltpu.VMEM((ORIENTS, 256, 256), BF),
            pltpu.VMEM((ORIENTS, 256, 256), BF),
            pltpu.VMEM((128, 32), F32),
            pltpu.VMEM((ORIENTS, EDGE, REFS, PLANE), F32),
            pltpu.VMEM((256, ORIENTS * PLANE), BF),
            pltpu.VMEM((4, 2, SIDE, 32, 256), BF),
            pltpu.VMEM((4, SIDE, 32, 256), BF),
            pltpu.VMEM((4, SIDE, 32, 256), BF),
            pltpu.VMEM((TILES // 2, 32, 256), BF),
            pltpu.VMEM((REFS, 8, 128), F32),
            pltpu.VMEM((DEPTH, 8, 128), F32),
            pltpu.VMEM((TILES, 8, 128), F32),
            pltpu.VMEM((256, 128), F32),
            dma((6,)),
            dma((CHUNKS, 17)),
            dma((CHUNKS, 17)),
            dma((DEPTH,)),
            dma((DEPTH,)),
            dma((4,)),
            dma((4,)),
            dma((4, SIDE)),
            dma((TILES // 2,)),
            dma((DEPTH,)),
            dma((DEPTH,)),
            dma((TILES,)),
            dma((TILES,)),
        ],
        compiler_params=pltpu.CompilerParams(
            collective_id=0, has_side_effects=True, vmem_limit_bytes=56 * 1024 * 1024
        ),
    )(subvols, tomogram.reshape(1, rows), sharpness.reshape(1, rows), references, interp, weighting)
    return updated.reshape(1, voxels), posterior.T


def solution(mesh):
    in_specs = (
        P(("tile", "cls"), None),
        P(("tile", "cls"), None),
        P(("tile", "cls")),
        P("cls", None),
        P(),
        P("tile", None, None),
    )
    out_specs = (P("cls", None), P(("tile", "cls"), None))
    return jax.shard_map(shards, mesh=mesh, in_specs=in_specs, out_specs=out_specs, check_vma=False)
```
